256 devices in a mesh: gx: 16 (over x, y_hi, core), gy: 16 (over y_lo, z).
Axes of the slice: x: 4, y: 4 (y_hi: 2, y_lo: 2; y = y_hi * 2 + y_lo), z: 8, core: 2. Of those that a mesh axis runs over, the one named last changes fastest.
Arguments:
- state: float32 [8, 128, 32, 2048], P(None, 'gx', None, 'gy'), may hold values from -6 to 6
- shifts: int32 [2, 128], P(None, 'gx'), may hold values from 0 to 2047
- fracs: float32 [2, 128], P(None, 'gx'), may hold values from 0 to 1
- offsets: int32 [2], replicated, may hold values from 0 to 2047
- kappa: float32 [8], replicated, may hold values from 0.04 to 0.16
Outputs:
- evolved: float32 [8, 128, 32, 2048], P(None, 'gx', None, 'gy')
The draws below stay inside these ranges and needn't reach their ends.
All inputs are finite; a program needn't handle non-finite values.
Results may differ from the reference program's by a relative error of at most 0.00002.
Values sent between devices are 32-bit elements; how exact they have to be, the bound alone decides.
No kernel may reach another device: no remote copies, remote signals or barrier semaphores. Data moves between devices by JAX's collectives and lax.ppermute only.
A program may use at most 64 MiB of HBM per device.

```python
import math
import jax
import jax.numpy as jnp
from jax import lax

NVAR = 8
NZ = 32
STEPS = 2
NX = 128
NY = 2048


def set_ends(values, stream_key, least, largest):
    dims = values.shape
    spot = [jax.random.randint(jax.random.fold_in(stream_key, axis), (), 0, dims[axis]) for axis in range(len(dims))]
    values = values.at[tuple(spot)].set(least)
    longest = dims.index(max(dims))
    spot[longest] = (spot[longest] + 1) % dims[longest]
    return values.at[tuple(spot)].set(largest)


def block_levels(stream_key, extent, shards, low, high):
    factor_of = 1.0
    for axis_at, shards_of in shards:
        steps = jax.random.uniform(jax.random.fold_in(jax.random.fold_in(stream_key, 6), axis_at), (shards_of,), jnp.float32, low / len(shards), high / len(shards))
        factor_of = factor_of * jnp.repeat(jnp.exp(steps), extent[axis_at] // shards_of).reshape((-1,) + (1,) * (len(extent) - 1 - axis_at))
    return factor_of


def scatter_about(rng, extent, width, reach, cuts=(), kind=jnp.bfloat16):
    loudness = block_levels(rng, extent, cuts, -0.22, 0.18) if cuts else 1.0
    values = jax.random.normal(rng, extent, jnp.float32) * width * loudness
    return jnp.minimum(jnp.maximum(values, -reach), reach).astype(kind)


def setup_inputs(seed: int = 0) -> dict:
    key_list = jax.random.split(jax.random.key(seed), 6)
    return {
        "state": scatter_about(key_list[0], (NVAR, NX, NZ, NY), 1.0, 6.0, ((1, 16), (3, 16)), jnp.float32),
        "shifts": set_ends(jax.random.randint(key_list[1], (STEPS, NX), 0, NY), jax.random.fold_in(key_list[1], 1), 0, NY - 1).astype(jnp.int32),
        "fracs": jnp.clip(1.0 * jax.random.uniform(key_list[2], (STEPS, NX), jnp.float32) ** block_levels(key_list[2], (STEPS, NX), ((1, 16),), -0.2, 0.2), 0.0, 1.0),
        "offsets": jax.random.randint(key_list[3], (STEPS,), 0, NY).astype(jnp.int32),
        "kappa": jnp.clip(jnp.exp(jax.random.uniform(key_list[4], (NVAR,), jnp.float32, math.log(0.04), math.log(0.16))), 0.04, 0.16),
    }


spin_gain = 0.2
spin_drag = 0.05
tidal_gain = 0.3


def shift_column(column, offset, weight):
    nearer = jnp.roll(column, offset, axis=-1)
    farther = jnp.roll(column, offset + 1, axis=-1)
    return (1.0 - weight) * nearer + weight * farther


def diffuse(values, rate, shifted, weights, offset):
    advected = jax.vmap(shift_column)(values, shifted, weights)
    lower = jnp.roll(advected[NX - 1], offset, axis=-1)
    upper = jnp.roll(advected[0], -offset, axis=-1)
    radial_sum = jnp.concatenate([lower[None], advected[:-1]], axis=0) + jnp.concatenate([advected[1:], upper[None]], axis=0)
    azimuthal_sum = jnp.roll(advected, -1, axis=-1) + jnp.roll(advected, 1, axis=-1)
    vertical_sum = jnp.concatenate([advected[:, :1], advected[:, :-1]], axis=1) + jnp.concatenate([advected[:, 1:], advected[:, -1:]], axis=1)
    laplace = radial_sum + azimuthal_sum + vertical_sum - 6.0 * advected
    return advected + rate * laplace


def reference(state, shifts, fracs, offsets, kappa):
    current = state
    position = (jnp.arange(NX).astype(jnp.float32) + 0.5) / NX - 0.5
    position = position[:, None, None]
    for section in range(STEPS):
        shifted = shifts[section]
        weights = fracs[section]
        offset = offsets[section]

        def per_field(packed):
            return diffuse(packed[0], packed[1], shifted, weights, offset)

        mixed = lax.map(per_field, (current, kappa))
        density = mixed[0]
        radial_mom = mixed[1]
        azimuthal_mom = mixed[2]
        new_radial = radial_mom + spin_gain * azimuthal_mom + tidal_gain * position * density
        new_azimuthal = azimuthal_mom - spin_drag * radial_mom
        current = jnp.concatenate([density[None], new_radial[None], new_azimuthal[None], mixed[3:]], axis=0)
    return current
```

```python
import jax
import jax.numpy as jnp
from jax import lax
from jax.experimental import pallas as pl
from jax.experimental.pallas import tpu as pltpu
from jax.sharding import PartitionSpec as P

spin_gain = 0.2
spin_drag = 0.05
tidal_gain = 0.3

LANES = 128
BLOCKS = 16
COLS = 8
HALF_VARS = 4
LEVELS = 4
COL_ROWS = HALF_VARS * LEVELS
ROWS = COLS * COL_ROWS
RIM = ROWS // LEVELS
HALVES = 2
LEVEL_BLOCKS = 8

F32 = jnp.float32
VMEM = pl.BlockSpec(memory_space=pltpu.VMEM)
SMEM = pl.BlockSpec(memory_space=pltpu.SMEM)
PARAMS = pltpu.CompilerParams(vmem_limit_bytes=24 * 1024 * 1024)


def shape(*dims):
    return jax.ShapeDtypeStruct(dims, F32)


def cost(flops, moved):
    return pl.CostEstimate(flops=flops, bytes_accessed=moved, transcendentals=0)


def lane_index():
    return lax.broadcasted_iota(jnp.int32, (8, LANES), 1)


def row_index():
    return lax.broadcasted_iota(jnp.int32, (8, LANES), 0)


def rotated(block, earlier, amount, lanes):
    joined = jnp.where(lanes < LANES - amount, block, earlier)
    return pltpu.roll(joined, amount & (LANES - 1), 1)


def pack_kernel(state, out):
    for half in range(HALVES):
        for col in range(COLS):
            for pair in range(2):
                var = half * HALF_VARS + 2 * pair
                base = col * COL_ROWS + pair * 8
                for tile in range(LEVEL_BLOCKS // 2):
                    first = state[var, col, pl.ds(tile * 8, 8), :]
                    second = state[var + 1, col, pl.ds(tile * 8, 8), :]
                    dest = half * LEVEL_BLOCKS + 2 * tile
                    out[dest, pl.ds(base, 8), :] = jnp.concatenate([first[:4], second[:4]], axis=0)
                    out[dest + 1, pl.ds(base, 8), :] = jnp.concatenate([first[4:], second[4:]], axis=0)


def unpack_kernel(packed, out):
    for half in range(HALVES):
        for col in range(COLS):
            for pair in range(2):
                var = half * HALF_VARS + 2 * pair
                base = col * COL_ROWS + pair * 8
                for tile in range(LEVEL_BLOCKS // 2):
                    source = half * LEVEL_BLOCKS + 2 * tile
                    low = packed[source, pl.ds(base, 8), :]
                    high = packed[source + 1, pl.ds(base, 8), :]
                    out[var, col, pl.ds(tile * 8, 8), :] = jnp.concatenate([low[:4], high[:4]], axis=0)
                    out[var + 1, col, pl.ds(tile * 8, 8), :] = jnp.concatenate([low[4:], high[4:]], axis=0)


def advect(step, shifts, fracs, values, adv, col_low, col_high, level_low, level_high):
    lanes = lane_index()
    turns = [shifts[step, col] for col in range(COLS)]
    far = [fracs[step, col] for col in range(COLS)]
    near = [1.0 - weight for weight in far]

    def block_step(block, carry):
        for col in range(COLS):
            source = (block - turns[col] // LANES) & (BLOCKS - 1)
            before = (source - 1) & (BLOCKS - 1)
            rest = turns[col] & (LANES - 1)
            for pair in range(2):
                rows = pl.ds(col * COL_ROWS + pair * 8, 8)
                here = values[source, rows, :]
                earlier = values[before, rows, :]
                nearer = rotated(here, earlier, rest, lanes)
                farther = rotated(here, earlier, rest + 1, lanes)
                result = near[col] * nearer + far[col] * farther
                adv[block, rows, :] = result
                if col == 0:
                    col_low[block, pl.ds(pair * 8, 8), :] = result
                if col == COLS - 1:
                    col_high[block, pl.ds(pair * 8, 8), :] = result
        level_low[block] = adv[block, pl.ds(0, RIM, stride=LEVELS), :]
        level_high[block] = adv[block, pl.ds(LEVELS - 1, RIM, stride=LEVELS), :]
        return carry

    lax.fori_loop(0, BLOCKS, block_step, 0)


def ghost_roll(source, target, amount):
    lanes = lane_index()
    whole = amount // LANES
    rest = amount & (LANES - 1)

    def block_step(block, carry):
        here = (block - whole) & (BLOCKS - 1)
        before = (here - 1) & (BLOCKS - 1)
        for pair in range(2):
            rows = pl.ds(pair * 8, 8)
            target[block, rows, :] = rotated(source[here, rows, :], source[before, rows, :], rest, lanes)
        return carry

    lax.fori_loop(0, BLOCKS, block_step, 0)


def diffuse(step, place, offsets, kappa, adv, col_before, col_after, level_below, level_above, out,
            ghost_low, ghost_high, under, over):
    radial, half, vertical = place[0], place[1], place[2]
    total_y = BLOCKS * LANES
    offset = offsets[step]
    ghost_roll(col_before, ghost_low, jnp.where(radial == 0, offset, 0))
    ghost_roll(col_after, ghost_high, jnp.where(radial == place[3] - 1, (total_y - offset) & (total_y - 1), 0))
    lanes = lane_index()
    rows8 = row_index()
    level = rows8 & (LEVELS - 1)
    upper_rows = rows8 >= LEVELS
    bottom = level == 0
    top = level == LEVELS - 1
    rates = [
        jnp.where(upper_rows, kappa[half * HALF_VARS + 2 * pair + 1], kappa[half * HALF_VARS + 2 * pair])
        for pair in range(2)
    ]
    coupled = jnp.where(half == 0, 1.0, 0.0)
    gain = jnp.where(upper_rows, spin_gain * coupled, 0.0)
    drag = jnp.where(upper_rows, 0.0, -spin_drag * coupled)
    total_x = (place[3] * COLS).astype(F32)
    tides = []
    for col in range(COLS):
        position = ((radial * COLS + col).astype(F32) + 0.5) / total_x - 0.5
        tides.append(jnp.where(upper_rows, tidal_gain * position * coupled, 0.0))
    has_below = vertical > 0
    has_above = vertical < LEVEL_BLOCKS - 1

    def block_step(block, carry):
        after = (block + 1) & (BLOCKS - 1)
        before = (block - 1) & (BLOCKS - 1)
        low_rim = pl.ds(0, RIM, stride=LEVELS)
        high_rim = pl.ds(LEVELS - 1, RIM, stride=LEVELS)
        under[low_rim, :] = jnp.where(has_below, level_below[block], adv[block, low_rim, :])
        over[high_rim, :] = jnp.where(has_above, level_above[block], adv[block, high_rim, :])
        for col in range(COLS):
            mixed = []
            for pair in range(2):
                base = col * COL_ROWS + pair * 8
                rows = pl.ds(base, 8)
                value = adv[block, rows, :]
                if col > 0:
                    inner = adv[block, pl.ds(base - COL_ROWS, 8), :]
                else:
                    inner = ghost_low[block, pl.ds(pair * 8, 8), :]
                if col < COLS - 1:
                    outer = adv[block, pl.ds(base + COL_ROWS, 8), :]
                else:
                    outer = ghost_high[block, pl.ds(pair * 8, 8), :]
                prior = pltpu.roll(jnp.where(lanes < LANES - 1, value, adv[before, rows, :]), 1, 1)
                following = pltpu.roll(jnp.where(lanes >= 1, value, adv[after, rows, :]), LANES - 1, 1)
                lower = jnp.where(bottom, under[rows, :], pltpu.roll(value, 1, 0))
                upper = jnp.where(top, over[rows, :], pltpu.roll(value, 7, 0))
                laplace = (inner + outer) + (prior + following) + (lower + upper) - 6.0 * value
                mixed.append(value + rates[pair] * laplace)
            swapped = [pltpu.roll(part, 4, 0) for part in mixed]
            first = mixed[0] + gain * swapped[1] + tides[col] * swapped[0]
            second = mixed[1] + drag * swapped[0]
            out[block, pl.ds(col * COL_ROWS, 8), :] = first
            out[block, pl.ds(col * COL_ROWS + 8, 8), :] = second
        return carry

    lax.fori_loop(0, BLOCKS, block_step, 0)


def pack(state):
    return pl.pallas_call(
        pack_kernel,
        out_shape=shape(BLOCKS, ROWS, LANES),
        in_specs=[VMEM],
        out_specs=VMEM,
        compiler_params=PARAMS,
        name="pack",
    )(state)


def unpack(packed):
    return pl.pallas_call(
        unpack_kernel,
        out_shape=shape(HALVES * HALF_VARS, COLS, LEVELS * LEVEL_BLOCKS, LANES),
        in_specs=[VMEM],
        out_specs=VMEM,
        compiler_params=PARAMS,
        name="unpack",
    )(packed)


ADVECTED = (
    shape(BLOCKS, ROWS, LANES),
    shape(BLOCKS, COL_ROWS, LANES),
    shape(BLOCKS, COL_ROWS, LANES),
    shape(BLOCKS, RIM, LANES),
    shape(BLOCKS, RIM, LANES),
)
GHOSTS = [
    pltpu.VMEM((BLOCKS, COL_ROWS, LANES), F32),
    pltpu.VMEM((BLOCKS, COL_ROWS, LANES), F32),
    pltpu.VMEM((ROWS, LANES), F32),
    pltpu.VMEM((ROWS, LANES), F32),
]


def first_advect(step, shifts, fracs, values):
    def kernel(shifts, fracs, values, *outs):
        advect(step, shifts, fracs, values, *outs)

    return pl.pallas_call(
        kernel,
        out_shape=ADVECTED,
        in_specs=[SMEM, SMEM, VMEM],
        out_specs=(VMEM,) * 5,
        compiler_params=PARAMS,
        name="advect",
    )(shifts, fracs, values)


def diffuse_advect(step, place, offsets, kappa, shifts, fracs, adv, halos):
    def kernel(place, offsets, kappa, shifts, fracs, adv, h0, h1, h2, h3, o0, o1, o2, o3, o4,
               current, ghost_low, ghost_high, under, over):
        diffuse(step, place, offsets, kappa, adv, h0, h1, h2, h3, current, ghost_low, ghost_high, under, over)
        advect(step + 1, shifts, fracs, current, o0, o1, o2, o3, o4)

    return pl.pallas_call(
        kernel,
        out_shape=ADVECTED,
        in_specs=[SMEM] * 5 + [VMEM] * 5,
        out_specs=(VMEM,) * 5,
        scratch_shapes=[pltpu.VMEM((BLOCKS, ROWS, LANES), F32)] + GHOSTS,
        compiler_params=PARAMS,
        name="diffuse_advect",
    )(place, offsets, kappa, shifts, fracs, adv, *halos)


def last_diffuse(step, place, offsets, kappa, adv, halos):
    def kernel(place, offsets, kappa, adv, h0, h1, h2, h3, out, ghost_low, ghost_high, under, over):
        diffuse(step, place, offsets, kappa, adv, h0, h1, h2, h3, out, ghost_low, ghost_high, under, over)

    return pl.pallas_call(
        kernel,
        out_shape=shape(BLOCKS, ROWS, LANES),
        in_specs=[SMEM] * 3 + [VMEM] * 5,
        out_specs=VMEM,
        scratch_shapes=GHOSTS,
        compiler_params=PARAMS,
        name="last_diffuse",
    )(place, offsets, kappa, adv, *halos)


def exchange(rims):
    col_low, col_high, level_low, level_high = rims
    radial_size = lax.axis_size("gx")
    up = [(i, (i + 1) % radial_size) for i in range(radial_size)]
    down = [(target, source) for source, target in up]
    ring = [
        (half * LEVEL_BLOCKS + block, half * LEVEL_BLOCKS + (block + 1) % LEVEL_BLOCKS)
        for half in range(HALVES)
        for block in range(LEVEL_BLOCKS)
    ]
    back = [(target, source) for source, target in ring]
    level_below = lax.ppermute(level_high, "gy", ring)
    level_above = lax.ppermute(level_low, "gy", back)
    col_before = lax.ppermute(col_high, "gx", up)
    col_after = lax.ppermute(col_low, "gx", down)
    return col_before, col_after, level_below, level_above


def on_device(state, shifts, fracs, offsets, kappa):
    around = lax.axis_index("gy")
    place = jnp.stack(
        [
            lax.axis_index("gx"),
            around // LEVEL_BLOCKS,
            around % LEVEL_BLOCKS,
            jnp.int32(lax.axis_size("gx")),
        ]
    ).astype(jnp.int32)
    steps = shifts.shape[0]
    values = lax.all_to_all(pack(state), "gy", 0, 0, tiled=True)
    adv, *rims = first_advect(0, shifts, fracs, values)
    for step in range(steps - 1):
        adv, *rims = diffuse_advect(step, place, offsets, kappa, shifts, fracs, adv, exchange(rims))
    values = last_diffuse(steps - 1, place, offsets, kappa, adv, exchange(rims))
    return unpack(lax.all_to_all(values, "gy", 0, 0, tiled=True))


def solution(mesh):
    placed = (P(None, "gx", None, "gy"), P(None, "gx"), P(None, "gx"), P(), P())
    return jax.shard_map(
        on_device, mesh=mesh, in_specs=placed, out_specs=P(None, "gx", None, "gy"), check_vma=False
    )
```

```python
import jax
import jax.numpy as jnp
from jax import lax
from jax.experimental import pallas as pl
from jax.experimental.pallas import tpu as pltpu
from jax.sharding import PartitionSpec as P

spin_gain = 0.2
spin_drag = 0.05
tidal_gain = 0.3

LANES = 128
BLOCKS = 16
COLS = 8
HALF_VARS = 4
LEVELS = 4
COL_ROWS = HALF_VARS * LEVELS
ROWS = COLS * COL_ROWS
RIM = ROWS // LEVELS
HALVES = 2
LEVEL_BLOCKS = 8

F32 = jnp.float32
VMEM = pl.BlockSpec(memory_space=pltpu.VMEM)
SMEM = pl.BlockSpec(memory_space=pltpu.SMEM)
PARAMS = pltpu.CompilerParams(vmem_limit_bytes=24 * 1024 * 1024)


def shape(*dims):
    return jax.ShapeDtypeStruct(dims, F32)


def cost(flops, moved):
    return pl.CostEstimate(flops=flops, bytes_accessed=moved, transcendentals=0)


def lane_index():
    return lax.broadcasted_iota(jnp.int32, (8, LANES), 1)


def row_index():
    return lax.broadcasted_iota(jnp.int32, (8, LANES), 0)


def rotated(block, earlier, amount, lanes):
    joined = jnp.where(lanes < LANES - amount, block, earlier)
    return pltpu.roll(joined, amount & (LANES - 1), 1)


def pack_kernel(state, out):
    for half in range(HALVES):
        for col in range(COLS):
            for pair in range(2):
                var = half * HALF_VARS + 2 * pair
                base = col * COL_ROWS + pair * 8
                for tile in range(LEVEL_BLOCKS // 2):
                    first = state[var, col, pl.ds(tile * 8, 8), :]
                    second = state[var + 1, col, pl.ds(tile * 8, 8), :]
                    dest = half * LEVEL_BLOCKS + 2 * tile
                    out[dest, pl.ds(base, 8), :] = jnp.concatenate([first[:4], second[:4]], axis=0)
                    out[dest + 1, pl.ds(base, 8), :] = jnp.concatenate([first[4:], second[4:]], axis=0)


def unpack_kernel(packed, out):
    for half in range(HALVES):
        for col in range(COLS):
            for pair in range(2):
                var = half * HALF_VARS + 2 * pair
                base = col * COL_ROWS + pair * 8
                for tile in range(LEVEL_BLOCKS // 2):
                    source = half * LEVEL_BLOCKS + 2 * tile
                    low = packed[source, pl.ds(base, 8), :]
                    high = packed[source + 1, pl.ds(base, 8), :]
                    out[var, col, pl.ds(tile * 8, 8), :] = jnp.concatenate([low[:4], high[:4]], axis=0)
                    out[var + 1, col, pl.ds(tile * 8, 8), :] = jnp.concatenate([low[4:], high[4:]], axis=0)


def advect(step, shifts, fracs, values, adv, col_low, col_high, level_low, level_high):
    lanes = lane_index()
    turns = [shifts[step, col] for col in range(COLS)]
    far = [fracs[step, col] for col in range(COLS)]
    near = [1.0 - weight for weight in far]

    def block_step(block, carry):
        for col in range(COLS):
            source = (block - turns[col] // LANES) & (BLOCKS - 1)
            before = (source - 1) & (BLOCKS - 1)
            rest = turns[col] & (LANES - 1)
            for pair in range(2):
                rows = pl.ds(col * COL_ROWS + pair * 8, 8)
                here = values[source, rows, :]
                earlier = values[before, rows, :]
                nearer = rotated(here, earlier, rest, lanes)
                farther = rotated(here, earlier, rest + 1, lanes)
                result = near[col] * nearer + far[col] * farther
                adv[block, rows, :] = result
                if col == 0:
                    col_low[block, pl.ds(pair * 8, 8), :] = result
                if col == COLS - 1:
                    col_high[block, pl.ds(pair * 8, 8), :] = result
        level_low[block] = adv[block, pl.ds(0, RIM, stride=LEVELS), :]
        level_high[block] = adv[block, pl.ds(LEVELS - 1, RIM, stride=LEVELS), :]
        return carry

    lax.fori_loop(0, BLOCKS, block_step, 0, unroll=16)


def ghost_roll(source, target, amount):
    lanes = lane_index()
    whole = amount // LANES
    rest = amount & (LANES - 1)

    def block_step(block, carry):
        here = (block - whole) & (BLOCKS - 1)
        before = (here - 1) & (BLOCKS - 1)
        for pair in range(2):
            rows = pl.ds(pair * 8, 8)
            target[block, rows, :] = rotated(source[here, rows, :], source[before, rows, :], rest, lanes)
        return carry

    lax.fori_loop(0, BLOCKS, block_step, 0, unroll=16)


def diffuse(step, place, offsets, kappa, adv, col_before, col_after, level_below, level_above, out,
            ghost_low, ghost_high, under, over):
    radial, half, vertical = place[0], place[1], place[2]
    total_y = BLOCKS * LANES
    offset = offsets[step]
    ghost_roll(col_before, ghost_low, jnp.where(radial == 0, offset, 0))
    ghost_roll(col_after, ghost_high, jnp.where(radial == place[3] - 1, (total_y - offset) & (total_y - 1), 0))
    lanes = lane_index()
    rows8 = row_index()
    level = rows8 & (LEVELS - 1)
    upper_rows = rows8 >= LEVELS
    bottom = level == 0
    top = level == LEVELS - 1
    rates = [
        jnp.where(upper_rows, kappa[half * HALF_VARS + 2 * pair + 1], kappa[half * HALF_VARS + 2 * pair])
        for pair in range(2)
    ]
    coupled = jnp.where(half == 0, 1.0, 0.0)
    gain = jnp.where(upper_rows, spin_gain * coupled, 0.0)
    drag = jnp.where(upper_rows, 0.0, -spin_drag * coupled)
    total_x = (place[3] * COLS).astype(F32)
    tides = []
    for col in range(COLS):
        position = ((radial * COLS + col).astype(F32) + 0.5) / total_x - 0.5
        tides.append(jnp.where(upper_rows, tidal_gain * position * coupled, 0.0))
    has_below = vertical > 0
    has_above = vertical < LEVEL_BLOCKS - 1

    def block_step(block, carry):
        after = (block + 1) & (BLOCKS - 1)
        before = (block - 1) & (BLOCKS - 1)
        low_rim = pl.ds(0, RIM, stride=LEVELS)
        high_rim = pl.ds(LEVELS - 1, RIM, stride=LEVELS)
        under[low_rim, :] = jnp.where(has_below, level_below[block], adv[block, low_rim, :])
        over[high_rim, :] = jnp.where(has_above, level_above[block], adv[block, high_rim, :])
        for col in range(COLS):
            mixed = []
            for pair in range(2):
                base = col * COL_ROWS + pair * 8
                rows = pl.ds(base, 8)
                value = adv[block, rows, :]
                if col > 0:
                    inner = adv[block, pl.ds(base - COL_ROWS, 8), :]
                else:
                    inner = ghost_low[block, pl.ds(pair * 8, 8), :]
                if col < COLS - 1:
                    outer = adv[block, pl.ds(base + COL_ROWS, 8), :]
                else:
                    outer = ghost_high[block, pl.ds(pair * 8, 8), :]
                prior = pltpu.roll(jnp.where(lanes < LANES - 1, value, adv[before, rows, :]), 1, 1)
                following = pltpu.roll(jnp.where(lanes >= 1, value, adv[after, rows, :]), LANES - 1, 1)
                lower = jnp.where(bottom, under[rows, :], pltpu.roll(value, 1, 0))
                upper = jnp.where(top, over[rows, :], pltpu.roll(value, 7, 0))
                laplace = (inner + outer) + (prior + following) + (lower + upper) - 6.0 * value
                mixed.append(value + rates[pair] * laplace)
            swapped = [pltpu.roll(part, 4, 0) for part in mixed]
            first = mixed[0] + gain * swapped[1] + tides[col] * swapped[0]
            second = mixed[1] + drag * swapped[0]
            out[block, pl.ds(col * COL_ROWS, 8), :] = first
            out[block, pl.ds(col * COL_ROWS + 8, 8), :] = second
        return carry

    lax.fori_loop(0, BLOCKS, block_step, 0, unroll=16)


def pack(state):
    return pl.pallas_call(
        pack_kernel,
        out_shape=shape(BLOCKS, ROWS, LANES),
        in_specs=[VMEM],
        out_specs=VMEM,
        compiler_params=PARAMS,
        name="pack",
    )(state)


def unpack(packed):
    return pl.pallas_call(
        unpack_kernel,
        out_shape=shape(HALVES * HALF_VARS, COLS, LEVELS * LEVEL_BLOCKS, LANES),
        in_specs=[VMEM],
        out_specs=VMEM,
        compiler_params=PARAMS,
        name="unpack",
    )(packed)


ADVECTED = (
    shape(BLOCKS, ROWS, LANES),
    shape(BLOCKS, COL_ROWS, LANES),
    shape(BLOCKS, COL_ROWS, LANES),
    shape(BLOCKS, RIM, LANES),
    shape(BLOCKS, RIM, LANES),
)
GHOSTS = [
    pltpu.VMEM((BLOCKS, COL_ROWS, LANES), F32),
    pltpu.VMEM((BLOCKS, COL_ROWS, LANES), F32),
    pltpu.VMEM((ROWS, LANES), F32),
    pltpu.VMEM((ROWS, LANES), F32),
]


def first_advect(step, shifts, fracs, values):
    def kernel(shifts, fracs, values, *outs):
        advect(step, shifts, fracs, values, *outs)

    return pl.pallas_call(
        kernel,
        out_shape=ADVECTED,
        in_specs=[SMEM, SMEM, VMEM],
        out_specs=(VMEM,) * 5,
        compiler_params=PARAMS,
        name="advect",
    )(shifts, fracs, values)


def diffuse_advect(step, place, offsets, kappa, shifts, fracs, adv, halos):
    def kernel(place, offsets, kappa, shifts, fracs, adv, h0, h1, h2, h3, o0, o1, o2, o3, o4,
               current, ghost_low, ghost_high, under, over):
        diffuse(step, place, offsets, kappa, adv, h0, h1, h2, h3, current, ghost_low, ghost_high, under, over)
        advect(step + 1, shifts, fracs, current, o0, o1, o2, o3, o4)

    return pl.pallas_call(
        kernel,
        out_shape=ADVECTED,
        in_specs=[SMEM] * 5 + [VMEM] * 5,
        out_specs=(VMEM,) * 5,
        scratch_shapes=[pltpu.VMEM((BLOCKS, ROWS, LANES), F32)] + GHOSTS,
        compiler_params=PARAMS,
        name="diffuse_advect",
    )(place, offsets, kappa, shifts, fracs, adv, *halos)


def last_diffuse(step, place, offsets, kappa, adv, halos):
    def kernel(place, offsets, kappa, adv, h0, h1, h2, h3, out, ghost_low, ghost_high, under, over):
        diffuse(step, place, offsets, kappa, adv, h0, h1, h2, h3, out, ghost_low, ghost_high, under, over)

    return pl.pallas_call(
        kernel,
        out_shape=shape(BLOCKS, ROWS, LANES),
        in_specs=[SMEM] * 3 + [VMEM] * 5,
        out_specs=VMEM,
        scratch_shapes=GHOSTS,
        compiler_params=PARAMS,
        name="last_diffuse",
    )(place, offsets, kappa, adv, *halos)


def exchange(rims):
    col_low, col_high, level_low, level_high = rims
    radial_size = lax.axis_size("gx")
    up = [(i, (i + 1) % radial_size) for i in range(radial_size)]
    down = [(target, source) for source, target in up]
    ring = [
        (half * LEVEL_BLOCKS + block, half * LEVEL_BLOCKS + (block + 1) % LEVEL_BLOCKS)
        for half in range(HALVES)
        for block in range(LEVEL_BLOCKS)
    ]
    back = [(target, source) for source, target in ring]
    level_below = lax.ppermute(level_high, "gy", ring)
    level_above = lax.ppermute(level_low, "gy", back)
    col_before = lax.ppermute(col_high, "gx", up)
    col_after = lax.ppermute(col_low, "gx", down)
    return col_before, col_after, level_below, level_above


def on_device(state, shifts, fracs, offsets, kappa):
    around = lax.axis_index("gy")
    place = jnp.stack(
        [
            lax.axis_index("gx"),
            around // LEVEL_BLOCKS,
            around % LEVEL_BLOCKS,
            jnp.int32(lax.axis_size("gx")),
        ]
    ).astype(jnp.int32)
    steps = shifts.shape[0]
    values = lax.all_to_all(pack(state), "gy", 0, 0, tiled=True)
    adv, *rims = first_advect(0, shifts, fracs, values)
    for step in range(steps - 1):
        adv, *rims = diffuse_advect(step, place, offsets, kappa, shifts, fracs, adv, exchange(rims))
    values = last_diffuse(steps - 1, place, offsets, kappa, adv, exchange(rims))
    return unpack(lax.all_to_all(values, "gy", 0, 0, tiled=True))


def solution(mesh):
    placed = (P(None, "gx", None, "gy"), P(None, "gx"), P(None, "gx"), P(), P())
    return jax.shard_map(
        on_device, mesh=mesh, in_specs=placed, out_specs=P(None, "gx", None, "gy"), check_vma=False
    )
```

```python
import jax
import jax.numpy as jnp
from jax import lax
from jax.experimental import pallas as pl
from jax.experimental.pallas import tpu as pltpu
from jax.sharding import PartitionSpec as P

spin_gain = 0.2
spin_drag = 0.05
tidal_gain = 0.3

LANES = 128
BLOCKS = 16
COLS = 8
HALF_VARS = 4
LEVELS = 4
COL_ROWS = HALF_VARS * LEVELS
ROWS = COLS * COL_ROWS
RIM = ROWS // LEVELS
HALVES = 2
LEVEL_BLOCKS = 8
VARS = HALVES * HALF_VARS

F32 = jnp.float32
VMEM = pl.BlockSpec(memory_space=pltpu.VMEM)
PARAMS = pltpu.CompilerParams(vmem_limit_bytes=24 * 1024 * 1024)


def shape(*dims):
    return jax.ShapeDtypeStruct(dims, F32)


def lane_index():
    return lax.broadcasted_iota(jnp.int32, (8, LANES), 1)


def row_index():
    return lax.broadcasted_iota(jnp.int32, (8, LANES), 0)


def rotated(block, earlier, amount, lanes):
    joined = jnp.where(lanes < LANES - amount, block, earlier)
    return pltpu.roll(joined, amount & (LANES - 1), 1)


def pack_kernel(state, out):
    for half in range(HALVES):
        for col in range(COLS):
            for pair in range(2):
                var = half * HALF_VARS + 2 * pair
                base = col * COL_ROWS + pair * 8
                for tile in range(LEVEL_BLOCKS // 2):
                    first = state[var, col, pl.ds(tile * 8, 8), :]
                    second = state[var + 1, col, pl.ds(tile * 8, 8), :]
                    dest = half * LEVEL_BLOCKS + 2 * tile
                    out[dest, pl.ds(base, 8), :] = jnp.concatenate([first[:4], second[:4]], axis=0)
                    out[dest + 1, pl.ds(base, 8), :] = jnp.concatenate([first[4:], second[4:]], axis=0)


def unpack_kernel(packed, out):
    for half in range(HALVES):
        for col in range(COLS):
            for pair in range(2):
                var = half * HALF_VARS + 2 * pair
                base = col * COL_ROWS + pair * 8
                for tile in range(LEVEL_BLOCKS // 2):
                    source = half * LEVEL_BLOCKS + 2 * tile
                    low = packed[source, pl.ds(base, 8), :]
                    high = packed[source + 1, pl.ds(base, 8), :]
                    out[var, col, pl.ds(tile * 8, 8), :] = jnp.concatenate([low[:4], high[:4]], axis=0)
                    out[var + 1, col, pl.ds(tile * 8, 8), :] = jnp.concatenate([low[4:], high[4:]], axis=0)


def advect(step, place, offset, shifts, fracs, values, adv, col_near, col_far, level_near, level_far):
    lanes = lane_index()
    turns = [shifts[step, col] for col in range(COLS)]
    far = [fracs[step, col] for col in range(COLS)]
    near = [1.0 - weight for weight in far]
    radial, vertical = place[0], place[2]
    even = (radial & 1) == 0
    level_even = (vertical & 1) == 0
    for block in range(BLOCKS):
        for col in range(COLS):
            source = (block - turns[col] // LANES) & (BLOCKS - 1)
            before = (source - 1) & (BLOCKS - 1)
            rest = turns[col] & (LANES - 1)
            for pair in range(2):
                rows = pl.ds(col * COL_ROWS + pair * 8, 8)
                here = values[source, rows, :]
                earlier = values[before, rows, :]
                nearer = rotated(here, earlier, rest, lanes)
                farther = rotated(here, earlier, rest + 1, lanes)
                adv[block, rows, :] = near[col] * nearer + far[col] * farther
        low = adv[block, pl.ds(0, RIM, stride=LEVELS), :]
        high = adv[block, pl.ds(LEVELS - 1, RIM, stride=LEVELS), :]
        level_near[block] = jnp.where(level_even, high, low)
        level_far[block] = jnp.where(level_even, low, high)
        for pair in range(2):
            rows = pl.ds(pair * 8, 8)
            low = adv[block, rows, :]
            high = adv[block, pl.ds((COLS - 1) * COL_ROWS + pair * 8, 8), :]
            col_near[block, rows, :] = jnp.where(even, high, low)
    start = jnp.where(even, 0, (COLS - 1) * COL_ROWS)
    far_ghost(place, offset, -1, adv, start, col_far)


def far_ghost(place, offset, sign, source, start, target):
    radial, radial_size = place[0], place[3]
    lanes = lane_index()
    signed = jnp.where(radial == 0, sign, jnp.where(radial == radial_size - 1, -sign, 0))
    turn = (signed * offset) & (BLOCKS * LANES - 1)
    whole = turn // LANES
    rest = turn & (LANES - 1)
    for block in range(BLOCKS):
        here = (block - whole) & (BLOCKS - 1)
        before = (here - 1) & (BLOCKS - 1)
        for pair in range(2):
            rows = pl.ds(pl.multiple_of(start + pair * 8, 8), 8)
            target[block, pl.ds(pair * 8, 8), :] = rotated(source[here, rows, :], source[before, rows, :], rest, lanes)


def where_am_i():
    around = lax.axis_index("gy")
    return lax.axis_index("gx"), around // LEVEL_BLOCKS, around % LEVEL_BLOCKS, lax.axis_size("gx")


def prepare(place, kappa, coefs):
    radial, half = place[0], place[1]
    first_half = half == 0
    upper_rows = row_index() >= LEVELS
    for pair in range(2):
        lower, upper = [
            jnp.where(first_half, kappa[0, 2 * pair + var], kappa[0, HALF_VARS + 2 * pair + var]) for var in range(2)
        ]
        coefs[pair] = jnp.where(upper_rows, upper, lower)
    coupled = jnp.where(first_half, 1.0, 0.0)
    coefs[2] = jnp.where(upper_rows, spin_gain * coupled, 0.0)
    coefs[3] = jnp.where(upper_rows, 0.0, -spin_drag * coupled)
    total_x = float(place[3] * COLS)
    for col in range(COLS):
        position = ((radial * COLS + col).astype(F32) + 0.5) / total_x - 0.5
        coefs[4 + col] = jnp.where(upper_rows, tidal_gain * position * coupled, 0.0)


def diffuse(place, coefs, adv, col_near, col_far, level_near, level_far, out, under, over):
    radial, vertical = place[0], place[2]
    even = (radial & 1) == 0
    level_even = (vertical & 1) == 0
    lanes = lane_index()
    level = row_index() & (LEVELS - 1)
    bottom = level == 0
    top = level == LEVELS - 1
    rates = [coefs[0], coefs[1]]
    gain = coefs[2]
    drag = coefs[3]
    tides = [coefs[4 + col] for col in range(COLS)]
    has_below = vertical > 0
    has_above = vertical < LEVEL_BLOCKS - 1
    low_rim = pl.ds(0, RIM, stride=LEVELS)
    high_rim = pl.ds(LEVELS - 1, RIM, stride=LEVELS)

    for block in range(BLOCKS):
        after = (block + 1) % BLOCKS
        before = (block - 1) % BLOCKS
        below = jnp.where(level_even, level_far[block], level_near[block])
        above = jnp.where(level_even, level_near[block], level_far[block])
        under[block, low_rim, :] = jnp.where(has_below, below, adv[block, low_rim, :])
        over[block, high_rim, :] = jnp.where(has_above, above, adv[block, high_rim, :])
        for col in range(COLS):
            mixed = []
            for pair in range(2):
                base = col * COL_ROWS + pair * 8
                rows = pl.ds(base, 8)
                ghost = pl.ds(pair * 8, 8)
                value = adv[block, rows, :]
                if col > 0:
                    inner = adv[block, pl.ds(base - COL_ROWS, 8), :]
                else:
                    inner = jnp.where(even, col_far[block, ghost, :], col_near[block, ghost, :])
                if col < COLS - 1:
                    outer = adv[block, pl.ds(base + COL_ROWS, 8), :]
                else:
                    outer = jnp.where(even, col_near[block, ghost, :], col_far[block, ghost, :])
                prior = pltpu.roll(jnp.where(lanes < LANES - 1, value, adv[before, rows, :]), 1, 1)
                following = pltpu.roll(jnp.where(lanes >= 1, value, adv[after, rows, :]), LANES - 1, 1)
                lower = jnp.where(bottom, under[block, rows, :], pltpu.roll(value, 1, 0))
                upper = jnp.where(top, over[block, rows, :], pltpu.roll(value, 7, 0))
                laplace = (inner + outer) + (prior + following) + (lower + upper) - 6.0 * value
                mixed.append(value + rates[pair] * laplace)
            swapped = [pltpu.roll(part, 4, 0) for part in mixed]
            first = mixed[0] + gain * swapped[1] + tides[col] * swapped[0]
            second = mixed[1] + drag * swapped[0]
            out[block, pl.ds(col * COL_ROWS, 8), :] = first
            out[block, pl.ds(col * COL_ROWS + 8, 8), :] = second


def unpack(packed):
    return call(unpack_kernel, "unpack", shape(VARS, COLS, LEVELS * LEVEL_BLOCKS, LANES), packed)


ADVECTED = (
    shape(BLOCKS, ROWS, LANES),
    shape(BLOCKS, COL_ROWS, LANES),
    shape(BLOCKS, COL_ROWS, LANES),
    shape(BLOCKS, RIM, LANES),
    shape(BLOCKS, RIM, LANES),
)
RIMS = [pltpu.VMEM((BLOCKS, ROWS, LANES), F32)] * 2


def call(kernel, name, outs, *args, scratch=()):
    return pl.pallas_call(
        kernel,
        out_shape=outs,
        in_specs=[VMEM] * len(args),
        out_specs=jax.tree.map(lambda _: VMEM, outs),
        scratch_shapes=scratch,
        compiler_params=PARAMS,
        name=name,
    )(*args)


def pack(state):
    return call(pack_kernel, "pack", shape(BLOCKS, ROWS, LANES), state)


def first_advect(shifts, fracs, values):
    def kernel(shifts, fracs, values, *outs):
        advect(0, where_am_i(), 0, shifts[...], fracs[...], values, *outs)

    return call(kernel, "advect", ADVECTED, shifts, fracs, values)


def constants(after, offsets, kappa):
    def kernel(after, offsets, kappa, offsets_out, coefs):
        offsets_out[...] = offsets[...]
        prepare(where_am_i(), kappa[...], coefs)

    return pl.pallas_call(
        kernel,
        out_shape=(jax.ShapeDtypeStruct(offsets.shape, offsets.dtype), shape(4 + COLS, 8, LANES)),
        in_specs=[pl.BlockSpec(memory_space=pl.ANY), VMEM, VMEM],
        out_specs=(VMEM, VMEM),
        compiler_params=PARAMS,
        name="constants",
    )(after, offsets, kappa)


def diffuse_advect(offsets, coefs, shifts, fracs, adv, halos):
    def kernel(offsets, coefs, shifts, fracs, adv, h0, h1, h2, h3, o0, o1, o2, o3, o4, current, ghost, under, over):
        place = where_am_i()
        offsets = offsets[...]
        far_ghost(place, offsets[0, 0], 1, h1, 0, ghost)
        diffuse(place, coefs, adv, h0, ghost, h2, h3, current, under, over)
        advect(1, place, offsets[0, 1], shifts[...], fracs[...], current, o0, o1, o2, o3, o4)

    scratch = [pltpu.VMEM((BLOCKS, ROWS, LANES), F32), pltpu.VMEM((BLOCKS, COL_ROWS, LANES), F32)] + RIMS
    return call(
        kernel, "diffuse_advect", ADVECTED, offsets, coefs, shifts, fracs, adv, *halos, scratch=scratch
    )


def last_diffuse(coefs, adv, halos):
    def kernel(coefs, adv, h0, h1, h2, h3, out, under, over):
        diffuse(where_am_i(), coefs, adv, h0, h1, h2, h3, out, under, over)

    return call(kernel, "last_diffuse", shape(BLOCKS, ROWS, LANES), coefs, adv, *halos, scratch=RIMS)


def swaps(count, first):
    pairs = [(i % count, (i + 1) % count) for i in range(first, count, 2)]
    return pairs + [(target, source) for source, target in pairs]


def exchange(rims):
    col_near, col_far, level_near, level_far = rims
    radial_size = lax.axis_size("gx")
    level_pairs = [
        [
            (half * LEVEL_BLOCKS + source, half * LEVEL_BLOCKS + target)
            for half in range(HALVES)
            for source, target in swaps(LEVEL_BLOCKS, first)
        ]
        for first in range(2)
    ]
    level_near = lax.ppermute(level_near, "gy", level_pairs[0])
    level_far = lax.ppermute(level_far, "gy", level_pairs[1])
    col_near = lax.ppermute(col_near, "gx", swaps(radial_size, 0))
    col_far = lax.ppermute(col_far, "gx", swaps(radial_size, 1))
    return col_near, col_far, level_near, level_far


def on_device(state, shifts, fracs, offsets, kappa):
    values = lax.all_to_all(pack(state), "gy", 0, 0, tiled=True)
    adv, *rims = first_advect(shifts, fracs, values)
    offsets, coefs = constants(adv, offsets[None], kappa[None])
    adv, *rims = diffuse_advect(offsets, coefs, shifts, fracs, adv, exchange(rims))
    values = last_diffuse(coefs, adv, exchange(rims))
    return unpack(lax.all_to_all(values, "gy", 0, 0, tiled=True))


def solution(mesh):
    placed = (P(None, "gx", None, "gy"), P(None, "gx"), P(None, "gx"), P(), P())
    return jax.shard_map(
        on_device, mesh=mesh, in_specs=placed, out_specs=P(None, "gx", None, "gy"), check_vma=False
    )
```

```python
import jax
import jax.numpy as jnp
from jax import lax
from jax.experimental import pallas as pl
from jax.experimental.pallas import tpu as pltpu
from jax.sharding import PartitionSpec as P

spin_gain = 0.2
spin_drag = 0.05
tidal_gain = 0.3

LANES = 128
BLOCKS = 16
COLS = 8
HALF_VARS = 4
LEVELS = 4
COL_ROWS = HALF_VARS * LEVELS
ROWS = COLS * COL_ROWS
RIM = ROWS // LEVELS
HALVES = 2
LEVEL_BLOCKS = 8
VARS = HALVES * HALF_VARS
RIM_COEFS = 4 + COLS
COEFS = RIM_COEFS + 3 + COLS // 2

F32 = jnp.float32
VMEM = pl.BlockSpec(memory_space=pltpu.VMEM)
PARAMS = pltpu.CompilerParams(vmem_limit_bytes=24 * 1024 * 1024)


def shape(*dims):
    return jax.ShapeDtypeStruct(dims, F32)


def lane_index():
    return lax.broadcasted_iota(jnp.int32, (8, LANES), 1)


def row_index():
    return lax.broadcasted_iota(jnp.int32, (8, LANES), 0)


def rotated(block, earlier, amount, lanes):
    joined = jnp.where(lanes < LANES - amount, block, earlier)
    return pltpu.roll(joined, amount & (LANES - 1), 1)


def pack_kernel(state, out):
    for half in range(HALVES):
        for col in range(COLS):
            for pair in range(2):
                var = half * HALF_VARS + 2 * pair
                base = col * COL_ROWS + pair * 8
                for tile in range(LEVEL_BLOCKS // 2):
                    first = state[var, col, pl.ds(tile * 8, 8), :]
                    second = state[var + 1, col, pl.ds(tile * 8, 8), :]
                    dest = half * LEVEL_BLOCKS + 2 * tile
                    out[dest, pl.ds(base, 8), :] = jnp.concatenate([first[:4], second[:4]], axis=0)
                    out[dest + 1, pl.ds(base, 8), :] = jnp.concatenate([first[4:], second[4:]], axis=0)


def unpack_kernel(packed, out):
    for half in range(HALVES):
        for col in range(COLS):
            for pair in range(2):
                var = half * HALF_VARS + 2 * pair
                base = col * COL_ROWS + pair * 8
                for tile in range(LEVEL_BLOCKS // 2):
                    source = half * LEVEL_BLOCKS + 2 * tile
                    low = packed[source, pl.ds(base, 8), :]
                    high = packed[source + 1, pl.ds(base, 8), :]
                    out[var, col, pl.ds(tile * 8, 8), :] = jnp.concatenate([low[:4], high[:4]], axis=0)
                    out[var + 1, col, pl.ds(tile * 8, 8), :] = jnp.concatenate([low[4:], high[4:]], axis=0)


def advect(step, place, offset, shifts, fracs, values, adv, col_near, col_far, level_near, level_far):
    lanes = lane_index()
    turns = [shifts[step, col] for col in range(COLS)]
    far = [fracs[step, col] for col in range(COLS)]
    near = [1.0 - weight for weight in far]
    radial, vertical = place[0], place[2]
    even = (radial & 1) == 0
    level_even = (vertical & 1) == 0
    for block in range(BLOCKS):
        for col in range(COLS):
            source = (block - turns[col] // LANES) & (BLOCKS - 1)
            before = (source - 1) & (BLOCKS - 1)
            rest = turns[col] & (LANES - 1)
            for pair in range(2):
                rows = pl.ds(col * COL_ROWS + pair * 8, 8)
                here = values[source, rows, :]
                earlier = values[before, rows, :]
                nearer = rotated(here, earlier, rest, lanes)
                farther = rotated(here, earlier, rest + 1, lanes)
                adv[block, rows, :] = near[col] * nearer + far[col] * farther
        low = adv[block, pl.ds(0, RIM, stride=LEVELS), :]
        high = adv[block, pl.ds(LEVELS - 1, RIM, stride=LEVELS), :]
        level_near[block] = jnp.where(level_even, high, low)
        level_far[block] = jnp.where(level_even, low, high)
        for pair in range(2):
            rows = pl.ds(pair * 8, 8)
            low = adv[block, rows, :]
            high = adv[block, pl.ds((COLS - 1) * COL_ROWS + pair * 8, 8), :]
            col_near[block, rows, :] = jnp.where(even, high, low)
    start = jnp.where(even, 0, (COLS - 1) * COL_ROWS)
    far_ghost(place, offset, -1, adv, start, col_far)


def far_ghost(place, offset, sign, source, start, target):
    radial, radial_size = place[0], place[3]
    lanes = lane_index()
    signed = jnp.where(radial == 0, sign, jnp.where(radial == radial_size - 1, -sign, 0))
    turn = (signed * offset) & (BLOCKS * LANES - 1)
    whole = turn // LANES
    rest = turn & (LANES - 1)
    for block in range(BLOCKS):
        here = (block - whole) & (BLOCKS - 1)
        before = (here - 1) & (BLOCKS - 1)
        for pair in range(2):
            rows = pl.ds(pl.multiple_of(start + pair * 8, 8), 8)
            target[block, pl.ds(pair * 8, 8), :] = rotated(source[here, rows, :], source[before, rows, :], rest, lanes)


def where_am_i():
    around = lax.axis_index("gy")
    return lax.axis_index("gx"), around // LEVEL_BLOCKS, around % LEVEL_BLOCKS, lax.axis_size("gx")


def prepare(place, kappa, coefs):
    radial, half, vertical = place[0], place[1], place[2]
    var = row_index() & (HALF_VARS - 1)
    first_half = half == 0
    upper_rows = row_index() >= LEVELS
    for pair in range(2):
        lower, upper = [
            jnp.where(first_half, kappa[0, 2 * pair + var], kappa[0, HALF_VARS + 2 * pair + var]) for var in range(2)
        ]
        coefs[pair] = jnp.where(upper_rows, upper, lower)
    coupled = jnp.where(first_half, 1.0, 0.0)
    coefs[2] = jnp.where(upper_rows, spin_gain * coupled, 0.0)
    coefs[3] = jnp.where(upper_rows, 0.0, -spin_drag * coupled)
    total_x = float(place[3] * COLS)
    for col in range(COLS):
        position = ((radial * COLS + col).astype(F32) + 0.5) / total_x - 0.5
        tide = tidal_gain * position * coupled
        coefs[4 + col] = jnp.where(upper_rows, tide, 0.0)
        turned = jnp.where(var == 1, tide, jnp.where(var == 2, -spin_drag * coupled, 0.0))
        if col % 2 == 0:
            earlier = turned
        else:
            coefs[RIM_COEFS + 3 + col // 2] = jnp.where(upper_rows, turned, earlier)
    rate = jnp.zeros((8, LANES), F32)
    for index in range(HALF_VARS):
        own = jnp.where(first_half, kappa[0, index], kappa[0, HALF_VARS + index])
        rate = jnp.where(var == index, own, rate)
    coefs[RIM_COEFS] = jnp.where(vertical > 0, rate, 0.0)
    coefs[RIM_COEFS + 1] = jnp.where(vertical < LEVEL_BLOCKS - 1, rate, 0.0)
    coefs[RIM_COEFS + 2] = jnp.where(var == 1, spin_gain * coupled, 0.0)


def sourced(mixed, coefs, col):
    gain = coefs[2]
    drag = coefs[3]
    swapped = [pltpu.roll(part, 4, 0) for part in mixed]
    return mixed[0] + gain * swapped[1] + coefs[4 + col] * swapped[0], mixed[1] + drag * swapped[0]


def interior(place, coefs, adv, out):
    vertical = place[2]
    lanes = lane_index()
    level = row_index() & (LEVELS - 1)
    bottom = level == 0
    top = level == LEVELS - 1
    keep_low = jnp.where(vertical > 0, 0.0, 1.0)
    keep_high = jnp.where(vertical < LEVEL_BLOCKS - 1, 0.0, 1.0)
    rates = [coefs[0], coefs[1]]
    for block in range(BLOCKS):
        after = (block + 1) % BLOCKS
        before = (block - 1) % BLOCKS
        for col in range(COLS):
            mixed = []
            for pair in range(2):
                base = col * COL_ROWS + pair * 8
                rows = pl.ds(base, 8)
                value = adv[block, rows, :]
                beside = [
                    adv[block, pl.ds(base + side * COL_ROWS, 8), :] for side in (-1, 1) if 0 <= col + side < COLS
                ]
                prior = pltpu.roll(jnp.where(lanes < LANES - 1, value, adv[before, rows, :]), 1, 1)
                following = pltpu.roll(jnp.where(lanes >= 1, value, adv[after, rows, :]), LANES - 1, 1)
                lower = jnp.where(bottom, keep_low * value, pltpu.roll(value, 1, 0))
                upper = jnp.where(top, keep_high * value, pltpu.roll(value, 7, 0))
                laplace = sum(beside[1:], beside[0]) + (prior + following) + (lower + upper) - 6.0 * value
                mixed.append(value + rates[pair] * laplace)
            first, second = sourced(mixed, coefs, col)
            out[block, pl.ds(col * COL_ROWS, 8), :] = first
            out[block, pl.ds(col * COL_ROWS + 8, 8), :] = second


def add_rims(place, coefs, inside, col_near, col_far, level_near, level_far, out):
    even = (place[0] & 1) == 0
    level_even = (place[2] & 1) == 0
    rates = [coefs[0], coefs[1]]
    onward = coefs[RIM_COEFS + 2]
    for block in range(BLOCKS):
        for col in range(COLS):
            parts = [inside[block, pl.ds(col * COL_ROWS + pair * 8, 8), :] for pair in range(2)]
            if col in (0, COLS - 1):
                nears = [col_near[block, pl.ds(pair * 8, 8), :] for pair in range(2)]
                fars = [col_far[block, pl.ds(pair * 8, 8), :] for pair in range(2)]
                far_here = even if col == 0 else jnp.logical_not(even)
                ghosts = [rates[pair] * jnp.where(far_here, fars[pair], nears[pair]) for pair in range(2)]
                parts = [part + extra for part, extra in zip(parts, sourced(ghosts, coefs, col))]
            for pair in range(2):
                out[block, pl.ds(col * COL_ROWS + pair * 8, 8), :] = parts[pair]
        for two in range(COLS // 2):
            rows = pl.ds(two * 8, 8)
            near = level_near[block, rows, :]
            far = level_far[block, rows, :]
            for edge, rim in ((0, jnp.where(level_even, far, near)), (1, jnp.where(level_even, near, far))):
                rim = coefs[RIM_COEFS + edge] * rim
                extra = (
                    rim
                    + onward * pltpu.roll(rim, 7, 0)
                    + coefs[RIM_COEFS + 3 + two] * pltpu.roll(rim, 1, 0)
                )
                strided = pl.ds(two * 2 * COL_ROWS + edge * (LEVELS - 1), 8, stride=LEVELS)
                out[block, strided, :] = out[block, strided, :] + extra


def unpack(packed):
    return call(unpack_kernel, "unpack", shape(VARS, COLS, LEVELS * LEVEL_BLOCKS, LANES), packed)


ADVECTED = (
    shape(BLOCKS, ROWS, LANES),
    shape(BLOCKS, COL_ROWS, LANES),
    shape(BLOCKS, COL_ROWS, LANES),
    shape(BLOCKS, RIM, LANES),
    shape(BLOCKS, RIM, LANES),
)
def call(kernel, name, outs, *args, scratch=()):
    return pl.pallas_call(
        kernel,
        out_shape=outs,
        in_specs=[VMEM] * len(args),
        out_specs=jax.tree.map(lambda _: VMEM, outs),
        scratch_shapes=scratch,
        compiler_params=PARAMS,
        name=name,
    )(*args)


def pack(state):
    return call(pack_kernel, "pack", shape(BLOCKS, ROWS, LANES), state)


def first_advect(shifts, fracs, values):
    def kernel(shifts, fracs, values, *outs):
        advect(0, where_am_i(), 0, shifts[...], fracs[...], values, *outs)

    return call(kernel, "advect", ADVECTED, shifts, fracs, values)


def first_interior(offsets, kappa, adv):
    def kernel(offsets, kappa, adv, offsets_out, coefs, out):
        place = where_am_i()
        offsets_out[...] = offsets[...]
        prepare(place, kappa[...], coefs)
        interior(place, coefs, adv, out)

    outs = (
        jax.ShapeDtypeStruct(offsets.shape, offsets.dtype),
        shape(COEFS, 8, LANES),
        shape(BLOCKS, ROWS, LANES),
    )
    return call(kernel, "interior", outs, offsets, kappa, adv)


def rims_advect(offsets, coefs, shifts, fracs, inside, halos):
    def kernel(offsets, coefs, shifts, fracs, inside, h0, h1, h2, h3, o0, o1, o2, o3, o4, current, ghost):
        place = where_am_i()
        offsets = offsets[...]
        far_ghost(place, offsets[0, 0], 1, h1, 0, ghost)
        add_rims(place, coefs, inside, h0, ghost, h2, h3, current)
        advect(1, place, offsets[0, 1], shifts[...], fracs[...], current, o0, o1, o2, o3, o4)

    scratch = [pltpu.VMEM((BLOCKS, ROWS, LANES), F32), pltpu.VMEM((BLOCKS, COL_ROWS, LANES), F32)]
    return call(
        kernel, "rims_advect", ADVECTED, offsets, coefs, shifts, fracs, inside, *halos, scratch=scratch
    )


def last_interior(coefs, adv):
    def kernel(coefs, adv, out):
        interior(where_am_i(), coefs, adv, out)

    return call(kernel, "last_interior", shape(BLOCKS, ROWS, LANES), coefs, adv)


def last_rims(coefs, inside, halos):
    def kernel(coefs, inside, h0, h1, h2, h3, out):
        add_rims(where_am_i(), coefs, inside, h0, h1, h2, h3, out)

    return call(kernel, "last_rims", shape(BLOCKS, ROWS, LANES), coefs, inside, *halos)


def swaps(count, first):
    pairs = [(i % count, (i + 1) % count) for i in range(first, count, 2)]
    return pairs + [(target, source) for source, target in pairs]


def exchange(rims):
    col_near, col_far, level_near, level_far = rims
    radial_size = lax.axis_size("gx")
    level_pairs = [
        [
            (half * LEVEL_BLOCKS + source, half * LEVEL_BLOCKS + target)
            for half in range(HALVES)
            for source, target in swaps(LEVEL_BLOCKS, first)
        ]
        for first in range(2)
    ]
    level_near = lax.ppermute(level_near, "gy", level_pairs[0])
    level_far = lax.ppermute(level_far, "gy", level_pairs[1])
    col_near = lax.ppermute(col_near, "gx", swaps(radial_size, 0))
    col_far = lax.ppermute(col_far, "gx", swaps(radial_size, 1))
    return col_near, col_far, level_near, level_far


def on_device(state, shifts, fracs, offsets, kappa):
    values = lax.all_to_all(pack(state), "gy", 0, 0, tiled=True)
    adv, *rims = first_advect(shifts, fracs, values)
    halos = exchange(rims)
    offsets, coefs, inside = first_interior(offsets[None], kappa[None], adv)
    adv, *rims = rims_advect(offsets, coefs, shifts, fracs, inside, halos)
    halos = exchange(rims)
    inside = last_interior(coefs, adv)
    values = last_rims(coefs, inside, halos)
    return unpack(lax.all_to_all(values, "gy", 0, 0, tiled=True))


def solution(mesh):
    placed = (P(None, "gx", None, "gy"), P(None, "gx"), P(None, "gx"), P(), P())
    return jax.shard_map(
        on_device, mesh=mesh, in_specs=placed, out_specs=P(None, "gx", None, "gy"), check_vma=False
    )
```

```python
import math
import jax
import jax.numpy as jnp
from jax import lax
from jax.experimental import pallas as pl
from jax.experimental.pallas import tpu as pltpu
from jax.sharding import PartitionSpec as P

spin_gain = 0.2
spin_drag = 0.05
tidal_gain = 0.3

LANES = 128
BLOCKS = 16
COLS = 8
HALF_VARS = 4
MODES = 4
COL_ROWS = HALF_VARS * MODES
ROWS = COLS * COL_ROWS
HALVES = 2
MODE_BLOCKS = 8
NZ = MODES * MODE_BLOCKS
VARS = HALVES * HALF_VARS
LAST = COLS - 1
EDGES = (0, LAST)
EDGE_ROWS = len(EDGES) * COL_ROWS
INNER_ROWS = ROWS - EDGE_ROWS
CENTERS = 4 + COLS
COEFS = CENTERS + 2

F32 = jnp.float32
VMEM = pl.BlockSpec(memory_space=pltpu.VMEM)
PARAMS = pltpu.CompilerParams(vmem_limit_bytes=28 * 1024 * 1024)


def shape(*dims):
    return jax.ShapeDtypeStruct(dims, F32)


def lane_index():
    return lax.broadcasted_iota(jnp.int32, (8, LANES), 1)


def row_index():
    return lax.broadcasted_iota(jnp.int32, (8, LANES), 0)


def rotated(block, earlier, amount, lanes):
    joined = jnp.where(lanes < LANES - amount, block, earlier)
    return pltpu.roll(joined, amount & (LANES - 1), 1)


def cosine(angle, mode):
    size = jnp.where(mode == 0, (1.0 / NZ) ** 0.5, (2.0 / NZ) ** 0.5)
    return size * jnp.cos((angle & (4 * NZ - 1)).astype(F32) * (math.pi / (2 * NZ)))


def to_modes(transposed):
    dims = (HALF_VARS * NZ, HALF_VARS * NZ)
    row = lax.broadcasted_iota(jnp.int32, dims, 1 if transposed else 0)
    column = lax.broadcasted_iota(jnp.int32, dims, 0 if transposed else 1)
    mode = (row // COL_ROWS) * MODES + row % MODES
    level = column % NZ
    same = (row // MODES) % HALF_VARS == column // NZ
    return jnp.where(same, cosine((2 * level + 1) * mode, mode), 0.0)


def exact_dot(left, right):
    return lax.dot(left, right, precision=lax.Precision.HIGHEST, preferred_element_type=F32)


def pack_kernel(state, out):
    basis = to_modes(False)
    for half in range(HALVES):
        for col in range(COLS):
            levels = jnp.concatenate([state[half * HALF_VARS + var, col] for var in range(HALF_VARS)], axis=0)
            modes = exact_dot(basis, levels)
            for block in range(MODE_BLOCKS):
                out[half * MODE_BLOCKS + block, col * COL_ROWS : (col + 1) * COL_ROWS, :] = modes[
                    block * COL_ROWS : (block + 1) * COL_ROWS
                ]


def unpack_kernel(back, packed, out):
    basis = back[...]
    for half in range(HALVES):
        for col in range(COLS):
            modes = jnp.concatenate(
                [
                    packed[half * MODE_BLOCKS + block, col * COL_ROWS : (col + 1) * COL_ROWS, :]
                    for block in range(MODE_BLOCKS)
                ],
                axis=0,
            )
            levels = exact_dot(basis, modes)
            for var in range(HALF_VARS):
                out[half * HALF_VARS + var, col] = levels[var * NZ : (var + 1) * NZ]


def mover(step, shifts, fracs):
    lanes = lane_index()
    turns = [shifts[step, col] for col in range(COLS)]
    far = [fracs[step, col] for col in range(COLS)]
    near = [1.0 - weight for weight in far]

    def move(values, block, start, col):
        source = (block - turns[col] // LANES) & (BLOCKS - 1)
        before = (source - 1) & (BLOCKS - 1)
        rest = turns[col] & (LANES - 1)
        rows = pl.ds(start, 8)
        here = values[source, rows, :]
        earlier = values[before, rows, :]
        nearer = rotated(here, earlier, rest, lanes)
        farther = rotated(here, earlier, rest + 1, lanes)
        return near[col] * nearer + far[col] * farther

    return move


def is_even(place):
    return (place[0] & 1) == 0


def far_ghost(place, offset, sign, source, start, target):
    radial, radial_size = place[0], place[3]
    lanes = lane_index()
    signed = jnp.where(radial == 0, sign, jnp.where(radial == radial_size - 1, -sign, 0))
    turn = (signed * offset) & (BLOCKS * LANES - 1)
    whole = turn // LANES
    rest = turn & (LANES - 1)
    for block in range(BLOCKS):
        here = (block - whole) & (BLOCKS - 1)
        before = (here - 1) & (BLOCKS - 1)
        for pair in range(2):
            rows = pl.ds(pl.multiple_of(start + pair * 8, 8), 8)
            target[block, pl.ds(pair * 8, 8), :] = rotated(source[here, rows, :], source[before, rows, :], rest, lanes)


def where_am_i():
    around = lax.axis_index("gy")
    return lax.axis_index("gx"), around // MODE_BLOCKS, around % MODE_BLOCKS, lax.axis_size("gx")


def prepare(place, kappa, coefs):
    radial, half, vertical = place[0], place[1], place[2]
    first_half = half == 0
    row = row_index()
    upper_rows = row >= MODES
    mode = vertical * MODES + (row & (MODES - 1))
    own = 2.0 * jnp.cos(mode.astype(F32) * (math.pi / NZ)) - 6.0
    for pair in range(2):
        lower, upper = [
            jnp.where(first_half, kappa[0, 2 * pair + var], kappa[0, HALF_VARS + 2 * pair + var]) for var in range(2)
        ]
        rate = jnp.where(upper_rows, upper, lower)
        coefs[pair] = rate
        coefs[CENTERS + pair] = 1.0 + rate * own
    coupled = jnp.where(first_half, 1.0, 0.0)
    coefs[2] = jnp.where(upper_rows, spin_gain * coupled, 0.0)
    coefs[3] = jnp.where(upper_rows, 0.0, -spin_drag * coupled)
    total_x = float(place[3] * COLS)
    for col in range(COLS):
        position = ((radial * COLS + col).astype(F32) + 0.5) / total_x - 0.5
        coefs[4 + col] = jnp.where(upper_rows, tidal_gain * position * coupled, 0.0)


def sourced(mixed, coefs, col):
    gain = coefs[2]
    drag = coefs[3]
    swapped = [pltpu.roll(part, 4, 0) for part in mixed]
    return mixed[0] + gain * swapped[1] + coefs[4 + col] * swapped[0], mixed[1] + drag * swapped[0]


def interior(coefs, adv, out):
    lanes = lane_index()
    for block in range(BLOCKS):
        after = (block + 1) % BLOCKS
        before = (block - 1) % BLOCKS
        for col in range(COLS):
            mixed = []
            for pair in range(2):
                base = col * COL_ROWS + pair * 8
                rows = pl.ds(base, 8)
                value = adv[block, rows, :]
                beside = [
                    adv[block, pl.ds(base + side * COL_ROWS, 8), :] for side in (-1, 1) if 0 <= col + side < COLS
                ]
                prior = pltpu.roll(jnp.where(lanes < LANES - 1, value, adv[before, rows, :]), 1, 1)
                following = pltpu.roll(jnp.where(lanes >= 1, value, adv[after, rows, :]), LANES - 1, 1)
                around = sum(beside[1:], beside[0]) + (prior + following)
                mixed.append(coefs[CENTERS + pair] * value + coefs[pair] * around)
            first, second = sourced(mixed, coefs, col)
            out[block, pl.ds(col * COL_ROWS, 8), :] = first
            out[block, pl.ds(col * COL_ROWS + 8, 8), :] = second


def with_ghosts(place, coefs, parts, near, far, block, col):
    even = is_even(place)
    far_here = even if col == 0 else jnp.logical_not(even)
    ghosts = [
        coefs[pair] * jnp.where(far_here, far[block, pl.ds(pair * 8, 8), :], near[block, pl.ds(pair * 8, 8), :])
        for pair in range(2)
    ]
    return [part + extra for part, extra in zip(parts, sourced(ghosts, coefs, col))]


def advect_edges_kernel(shifts, fracs, values, edges, near, far):
    even = is_even(where_am_i())
    move = mover(0, shifts[...], fracs[...])
    for block in range(BLOCKS):
        for pair in range(2):
            low, high = [move(values, block, col * COL_ROWS + pair * 8, col) for col in EDGES]
            rows = pl.ds(pair * 8, 8)
            edges[block, rows, :] = low
            edges[block, pl.ds(COL_ROWS + pair * 8, 8), :] = high
            near[block, rows, :] = jnp.where(even, high, low)
            far[block, rows, :] = jnp.where(even, low, high)


def inner_kernel(offsets, kappa, shifts, fracs, values, edges, offsets_out, coefs, back, inner, partial, adv, current):
    offsets_out[...] = offsets[...]
    back[...] = to_modes(True)
    prepare(where_am_i(), kappa[...], coefs)
    shifts = shifts[...]
    fracs = fracs[...]
    move = mover(0, shifts, fracs)
    for block in range(BLOCKS):
        adv[block, pl.ds(0, COL_ROWS), :] = edges[block, pl.ds(0, COL_ROWS), :]
        adv[block, pl.ds(LAST * COL_ROWS, COL_ROWS), :] = edges[block, pl.ds(COL_ROWS, COL_ROWS), :]
        for col in range(1, LAST):
            for pair in range(2):
                start = col * COL_ROWS + pair * 8
                adv[block, pl.ds(start, 8), :] = move(values, block, start, col)
    interior(coefs, adv, current)
    move = mover(1, shifts, fracs)
    for block in range(BLOCKS):
        partial[block, pl.ds(0, COL_ROWS), :] = current[block, pl.ds(0, COL_ROWS), :]
        partial[block, pl.ds(COL_ROWS, COL_ROWS), :] = current[block, pl.ds(LAST * COL_ROWS, COL_ROWS), :]
        for col in range(1, LAST):
            for pair in range(2):
                start = col * COL_ROWS + pair * 8
                inner[block, pl.ds(start - COL_ROWS, 8), :] = move(current, block, start, col)


def edges_kernel(offsets, coefs, shifts, fracs, partial, col_near, col_far, edges, near, far, ghost, whole):
    place = where_am_i()
    even = is_even(place)
    offsets = offsets[...]
    far_ghost(place, offsets[0, 0], 1, col_far, 0, ghost)
    for block in range(BLOCKS):
        for side, col in enumerate(EDGES):
            rows = [pl.ds(side * COL_ROWS + pair * 8, 8) for pair in range(2)]
            parts = [partial[block, row, :] for row in rows]
            for row, part in zip(rows, with_ghosts(place, coefs, parts, col_near, ghost, block, col)):
                whole[block, row, :] = part
    move = mover(1, shifts[...], fracs[...])
    for block in range(BLOCKS):
        for pair in range(2):
            low, high = [move(whole, block, side * COL_ROWS + pair * 8, col) for side, col in enumerate(EDGES)]
            edges[block, pl.ds(pair * 8, 8), :] = low
            edges[block, pl.ds(COL_ROWS + pair * 8, 8), :] = high
            near[block, pl.ds(pair * 8, 8), :] = jnp.where(even, high, low)
    far_ghost(place, offsets[0, 1], -1, edges, jnp.where(even, 0, COL_ROWS), far)


def last_interior_kernel(coefs, inner, edges, out, adv):
    for block in range(BLOCKS):
        adv[block, pl.ds(0, COL_ROWS), :] = edges[block, pl.ds(0, COL_ROWS), :]
        adv[block, pl.ds(LAST * COL_ROWS, COL_ROWS), :] = edges[block, pl.ds(COL_ROWS, COL_ROWS), :]
        adv[block, pl.ds(COL_ROWS, INNER_ROWS), :] = inner[block]
    interior(coefs, adv, out)


def last_edges_kernel(coefs, inside, col_near, col_far, out):
    place = where_am_i()
    for block in range(BLOCKS):
        out[block, pl.ds(COL_ROWS, INNER_ROWS), :] = inside[block, pl.ds(COL_ROWS, INNER_ROWS), :]
        for col in EDGES:
            rows = [pl.ds(col * COL_ROWS + pair * 8, 8) for pair in range(2)]
            parts = [inside[block, row, :] for row in rows]
            for row, part in zip(rows, with_ghosts(place, coefs, parts, col_near, col_far, block, col)):
                out[block, row, :] = part


def call(kernel, name, outs, *args, scratch=()):
    return pl.pallas_call(
        kernel,
        out_shape=outs,
        in_specs=[VMEM] * len(args),
        out_specs=jax.tree.map(lambda _: VMEM, outs),
        scratch_shapes=scratch,
        compiler_params=PARAMS,
        name=name,
    )(*args)


def swaps(count, first):
    pairs = [(i % count, (i + 1) % count) for i in range(first, count, 2)]
    return pairs + [(target, source) for source, target in pairs]


def exchange(near, far):
    radial_size = lax.axis_size("gx")
    return lax.ppermute(near, "gx", swaps(radial_size, 0)), lax.ppermute(far, "gx", swaps(radial_size, 1))


def across(values):
    return lax.all_to_all(values, "gy", 0, 0, tiled=True)


def on_device(state, shifts, fracs, offsets, kappa):
    whole = shape(BLOCKS, ROWS, LANES)
    column = shape(BLOCKS, COL_ROWS, LANES)
    edge = shape(BLOCKS, EDGE_ROWS, LANES)
    offsets = offsets[None]
    kappa = kappa[None]
    values = across(call(pack_kernel, "pack", whole, state))
    edges, near, far = call(advect_edges_kernel, "advect_edges", (edge, column, column), shifts, fracs, values)
    halos = exchange(near, far)
    offsets, coefs, back, inner, partial = call(
        inner_kernel,
        "inner",
        (
            jax.ShapeDtypeStruct(offsets.shape, offsets.dtype),
            shape(COEFS, 8, LANES),
            shape(HALF_VARS * NZ, HALF_VARS * NZ),
            shape(BLOCKS, INNER_ROWS, LANES),
            edge,
        ),
        offsets,
        kappa,
        shifts,
        fracs,
        values,
        edges,
        scratch=[pltpu.VMEM((BLOCKS, ROWS, LANES), F32)] * 2,
    )
    edges, near, far = call(
        edges_kernel,
        "edges",
        (edge, column, column),
        offsets,
        coefs,
        shifts,
        fracs,
        partial,
        *halos,
        scratch=[pltpu.VMEM((BLOCKS, COL_ROWS, LANES), F32), pltpu.VMEM((BLOCKS, EDGE_ROWS, LANES), F32)],
    )
    halos = exchange(near, far)
    inside = call(
        last_interior_kernel,
        "last_interior",
        whole,
        coefs,
        inner,
        edges,
        scratch=[pltpu.VMEM((BLOCKS, ROWS, LANES), F32)],
    )
    values = across(call(last_edges_kernel, "last_edges", whole, coefs, inside, *halos))
    return call(unpack_kernel, "unpack", shape(VARS, COLS, NZ, LANES), back, values)


def solution(mesh):
    placed = (P(None, "gx", None, "gy"), P(None, "gx"), P(None, "gx"), P(), P())
    return jax.shard_map(
        on_device, mesh=mesh, in_specs=placed, out_specs=P(None, "gx", None, "gy"), check_vma=False
    )
```

```python
import math
import jax
import jax.numpy as jnp
from jax import lax
from jax.experimental import pallas as pl
from jax.experimental.pallas import tpu as pltpu
from jax.sharding import PartitionSpec as P

spin_gain = 0.2
spin_drag = 0.05
tidal_gain = 0.3

LANES = 128
BLOCKS = 16
COLS = 8
HALF_VARS = 4
MODES = 4
COL_ROWS = HALF_VARS * MODES
ROWS = COLS * COL_ROWS
HALVES = 2
MODE_BLOCKS = 8
NZ = MODES * MODE_BLOCKS
VARS = HALVES * HALF_VARS
LAST = COLS - 1
SIDE_ROWS = 2 * COL_ROWS
CENTERS = 4 + COLS
GHOST_TIDES = CENTERS + 2
COEFS = GHOST_TIDES + 2

F32 = jnp.float32
VMEM = pl.BlockSpec(memory_space=pltpu.VMEM)
PARAMS = pltpu.CompilerParams(vmem_limit_bytes=28 * 1024 * 1024)


def shape(*dims):
    return jax.ShapeDtypeStruct(dims, F32)


def lane_index():
    return lax.broadcasted_iota(jnp.int32, (8, LANES), 1)


def row_index():
    return lax.broadcasted_iota(jnp.int32, (8, LANES), 0)


def rotated(block, earlier, amount, lanes):
    joined = jnp.where(lanes < LANES - amount, block, earlier)
    return pltpu.roll(joined, amount & (LANES - 1), 1)


def cosine(angle, mode):
    size = jnp.where(mode == 0, (1.0 / NZ) ** 0.5, (2.0 / NZ) ** 0.5)
    return size * jnp.cos((angle & (4 * NZ - 1)).astype(F32) * (math.pi / (2 * NZ)))


def to_modes(transposed):
    dims = (HALF_VARS * NZ, HALF_VARS * NZ)
    row = lax.broadcasted_iota(jnp.int32, dims, 1 if transposed else 0)
    column = lax.broadcasted_iota(jnp.int32, dims, 0 if transposed else 1)
    mode = (row // COL_ROWS) * MODES + row % MODES
    level = column % NZ
    same = (row // MODES) % HALF_VARS == column // NZ
    return jnp.where(same, cosine((2 * level + 1) * mode, mode), 0.0)


def exact_dot(left, right):
    return lax.dot(left, right, precision=lax.Precision.HIGHEST, preferred_element_type=F32)


def pack_kernel(state, out):
    basis = to_modes(False)
    for half in range(HALVES):
        for col in range(COLS):
            levels = jnp.concatenate([state[half * HALF_VARS + var, col] for var in range(HALF_VARS)], axis=0)
            modes = exact_dot(basis, levels)
            for block in range(MODE_BLOCKS):
                out[half * MODE_BLOCKS + block, col * COL_ROWS : (col + 1) * COL_ROWS, :] = modes[
                    block * COL_ROWS : (block + 1) * COL_ROWS
                ]


def unpack_kernel(back, packed, out):
    basis = back[...]
    for half in range(HALVES):
        for col in range(COLS):
            modes = jnp.concatenate(
                [
                    packed[half * MODE_BLOCKS + block, col * COL_ROWS : (col + 1) * COL_ROWS, :]
                    for block in range(MODE_BLOCKS)
                ],
                axis=0,
            )
            levels = exact_dot(basis, modes)
            for var in range(HALF_VARS):
                out[half * HALF_VARS + var, col] = levels[var * NZ : (var + 1) * NZ]


def move(values, block, rows, turn, weight):
    source = (block - turn // LANES) & (BLOCKS - 1)
    before = (source - 1) & (BLOCKS - 1)
    rest = turn & (LANES - 1)
    lanes = lane_index()
    here = values[source, rows, :]
    earlier = values[before, rows, :]
    nearer = rotated(here, earlier, rest, lanes)
    farther = rotated(here, earlier, rest + 1, lanes)
    return (1.0 - weight) * nearer + weight * farther


def is_even(place):
    return (place[0] & 1) == 0


def turned(values, block, rows, turn):
    here = (block - turn // LANES) & (BLOCKS - 1)
    before = (here - 1) & (BLOCKS - 1)
    return rotated(values[here, rows, :], values[before, rows, :], turn & (LANES - 1), lane_index())


def where_am_i():
    around = lax.axis_index("gy")
    return lax.axis_index("gx"), around // MODE_BLOCKS, around % MODE_BLOCKS, lax.axis_size("gx")


def prepare(place, kappa, coefs):
    radial, half, vertical = place[0], place[1], place[2]
    first_half = half == 0
    row = row_index()
    upper_rows = row >= MODES
    mode = vertical * MODES + (row & (MODES - 1))
    own = 2.0 * jnp.cos(mode.astype(F32) * (math.pi / NZ)) - 6.0
    for pair in range(2):
        lower, upper = [
            jnp.where(first_half, kappa[0, 2 * pair + var], kappa[0, HALF_VARS + 2 * pair + var]) for var in range(2)
        ]
        rate = jnp.where(upper_rows, upper, lower)
        coefs[pair] = rate
        coefs[CENTERS + pair] = 1.0 + rate * own
    coupled = jnp.where(first_half, 1.0, 0.0)
    coefs[2] = jnp.where(upper_rows, spin_gain * coupled, 0.0)
    coefs[3] = jnp.where(upper_rows, 0.0, -spin_drag * coupled)
    total = place[3] * COLS
    columns = [(4 + col, radial * COLS + col) for col in range(COLS)]
    columns.append((GHOST_TIDES, jnp.where(radial == 0, total - 1, radial * COLS - 1)))
    columns.append((GHOST_TIDES + 1, jnp.where(radial == place[3] - 1, 0, radial * COLS + COLS)))
    for slot, column in columns:
        position = (column.astype(F32) + 0.5) / float(total) - 0.5
        coefs[slot] = jnp.where(upper_rows, tidal_gain * position * coupled, 0.0)


def sourced(mixed, coefs, tide):
    swapped = [pltpu.roll(part, 4, 0) for part in mixed]
    return mixed[0] + coefs[2] * swapped[1] + tide * swapped[0], mixed[1] + coefs[3] * swapped[0]


def around(values, block, rows):
    lanes = lane_index()
    value = values[block, rows, :]
    after = values[(block + 1) % BLOCKS, rows, :]
    before = values[(block - 1) % BLOCKS, rows, :]
    prior = pltpu.roll(jnp.where(lanes < LANES - 1, value, before), 1, 1)
    following = pltpu.roll(jnp.where(lanes >= 1, value, after), LANES - 1, 1)
    return prior + following


def tiles(start):
    return [pl.ds(start + pair * 8, 8) for pair in range(2)]


def interior(coefs, adv, block, col, low, high):
    mixed = []
    for pair, rows in enumerate(tiles(col * COL_ROWS)):
        beside = [
            adv[block, pl.ds((col + side) * COL_ROWS + pair * 8, 8), :]
            for side in (-1, 1)
            if low <= col + side <= high
        ]
        total = sum(beside[1:], beside[0]) + around(adv, block, rows)
        mixed.append(coefs[CENTERS + pair] * adv[block, rows, :] + coefs[pair] * total)
    return sourced(mixed, coefs, coefs[4 + col])


def advect_edges_kernel(shifts, fracs, values, edges, near, far):
    even = is_even(where_am_i())
    shifts = shifts[...]
    fracs = fracs[...]
    for block in range(BLOCKS):
        for depth in range(2):
            low_col, high_col = depth, LAST - depth
            for pair in range(2):
                low, high = [
                    move(values, block, pl.ds(col * COL_ROWS + pair * 8, 8), shifts[0, col], fracs[0, col])
                    for col in (low_col, high_col)
                ]
                start = depth * SIDE_ROWS + pair * 8
                edges[block, pl.ds(start, 8), :] = low
                edges[block, pl.ds(start + COL_ROWS, 8), :] = high
                rows = pl.ds(depth * COL_ROWS + pair * 8, 8)
                near[block, rows, :] = jnp.where(even, high, low)
                far[block, rows, :] = jnp.where(even, low, high)
    lanes = lane_index()
    low, high = [
        jnp.where(lanes == 0, shifts[1, col].astype(F32), jnp.where(lanes == 1, fracs[1, col], 0.0))
        for col in (0, LAST)
    ]
    for target, side in ((near, jnp.where(even, high, low)), (far, jnp.where(even, low, high))):
        target[BLOCKS] = jnp.zeros((SIDE_ROWS, LANES), F32)
        target[BLOCKS, pl.ds(0, 8), :] = side


def inner_kernel(offsets, kappa, shifts, fracs, values, edges, offsets_out, coefs, back, partial, beyond, unfinished,
                 middle, adv, current):
    offsets_out[...] = offsets[...]
    back[...] = to_modes(True)
    prepare(where_am_i(), kappa[...], coefs)
    shifts = shifts[...]
    fracs = fracs[...]
    for block in range(BLOCKS):
        for slot, col in enumerate((0, LAST, 1, LAST - 1)):
            adv[block, pl.ds(col * COL_ROWS, COL_ROWS), :] = edges[block, pl.ds(slot * COL_ROWS, COL_ROWS), :]
        for col in range(2, LAST - 1):
            for rows in tiles(col * COL_ROWS):
                adv[block, rows, :] = move(values, block, rows, shifts[0, col], fracs[0, col])
    for block in range(BLOCKS):
        for col in range(COLS):
            for rows, result in zip(tiles(col * COL_ROWS), interior(coefs, adv, block, col, 0, LAST)):
                current[block, rows, :] = result
        partial[block, pl.ds(0, COL_ROWS), :] = current[block, pl.ds(0, COL_ROWS), :]
        partial[block, pl.ds(COL_ROWS, COL_ROWS), :] = current[block, pl.ds(LAST * COL_ROWS, COL_ROWS), :]
    for block in range(BLOCKS):
        for col in range(1, LAST):
            for rows in tiles(col * COL_ROWS):
                adv[block, rows, :] = move(current, block, rows, shifts[1, col], fracs[1, col])
    for block in range(BLOCKS):
        for slot, col in enumerate((1, LAST - 1)):
            beyond[block, pl.ds(slot * COL_ROWS, COL_ROWS), :] = adv[block, pl.ds(col * COL_ROWS, COL_ROWS), :]
        for col in range(1, LAST):
            for pair, result in enumerate(interior(coefs, adv, block, col, 1, LAST - 1)):
                if col == 1:
                    unfinished[block, pl.ds(pair * 8, 8), :] = result
                elif col == LAST - 1:
                    unfinished[block, pl.ds(COL_ROWS + pair * 8, 8), :] = result
                else:
                    middle[block, pl.ds((col - 2) * COL_ROWS + pair * 8, 8), :] = result


def outer_kernel(offsets, coefs, shifts, fracs, edges, partial, beyond, unfinished, middle, near, far, out,
                 own, ghost, own_moved, ghost_moved):
    place = where_am_i()
    even = is_even(place)
    radial, radial_size = place[0], place[3]
    shifts = shifts[...]
    fracs = fracs[...]
    offsets = offsets[...]
    signed = jnp.where(radial == 0, 1, jnp.where(radial == radial_size - 1, -1, 0))
    total_y = BLOCKS * LANES

    def side_tiles(side, base=0):
        return [pl.ds(pl.multiple_of(base + side * COL_ROWS + pair * 8, 8), 8) for pair in range(2)]

    for index, (message, side) in enumerate(((near, jnp.where(even, 1, 0)), (far, jnp.where(even, 0, 1)))):
        crosses = index == 1
        slots = tiles(index * COL_ROWS)
        own_tide = coefs[4 + LAST * side]
        ghost_tide = coefs[GHOST_TIDES + side]
        next_tide = coefs[5 + (LAST - 2) * side]
        mine = side_tiles(side)
        scalars = message[BLOCKS, pl.ds(0, 8), :]
        ghost_turn = scalars.astype(jnp.int32)[0, 0]
        ghost_weight = scalars[0, 1]
        own_turn = jnp.where(side == 0, shifts[1, 0], shifts[1, LAST])
        own_weight = jnp.where(side == 0, fracs[1, 0], fracs[1, LAST])

        first_turn = (signed * offsets[0, 0]) & (total_y - 1)
        back_turn = (-signed * offsets[0, 0]) & (total_y - 1)
        for block in range(BLOCKS):
            arrived = []
            mixed = []
            for pair, rows in enumerate(tiles(0)):
                value = message[block, rows, :]
                if crosses:
                    incoming = turned(message, block, rows, first_turn)
                    outgoing = turned(edges, block, mine[pair], back_turn)
                else:
                    incoming = value
                    outgoing = edges[block, mine[pair], :]
                arrived.append(coefs[pair] * incoming)
                other = message[block, tiles(COL_ROWS)[pair], :]
                total = (other + outgoing) + around(message, block, rows)
                mixed.append(coefs[CENTERS + pair] * value + coefs[pair] * total)
            for pair, extra in enumerate(sourced(arrived, coefs, own_tide)):
                own[block, slots[pair], :] = partial[block, mine[pair], :] + extra
            for pair, result in enumerate(sourced(mixed, coefs, ghost_tide)):
                ghost[block, slots[pair], :] = result
        for block in range(BLOCKS):
            for rows in slots:
                own_moved[block, rows, :] = move(own, block, rows, own_turn, own_weight)
                ghost_moved[block, rows, :] = move(ghost, block, rows, ghost_turn, ghost_weight)
        last_turn = (signed * offsets[0, 1]) & (total_y - 1)
        own_out = [
            pl.ds(pl.multiple_of(LAST * COL_ROWS * side + pair * 8, 8), 8) for pair in range(2)
        ]
        next_out = [
            pl.ds(pl.multiple_of(COL_ROWS + (LAST - 2) * COL_ROWS * side + pair * 8, 8), 8) for pair in range(2)
        ]
        for block in range(BLOCKS):
            mixed = []
            arrived = []
            for pair, rows in enumerate(slots):
                value = own_moved[block, rows, :]
                if crosses:
                    incoming = turned(ghost_moved, block, rows, last_turn)
                else:
                    incoming = ghost_moved[block, rows, :]
                total = (incoming + beyond[block, mine[pair], :]) + around(own_moved, block, rows)
                mixed.append(coefs[CENTERS + pair] * value + coefs[pair] * total)
                arrived.append(coefs[pair] * value)
            for pair, result in enumerate(sourced(mixed, coefs, own_tide)):
                out[block, own_out[pair], :] = result
            for pair, extra in enumerate(sourced(arrived, coefs, next_tide)):
                out[block, next_out[pair], :] = unfinished[block, mine[pair], :] + extra
    for block in range(BLOCKS):
        out[block, pl.ds(SIDE_ROWS, 4 * COL_ROWS), :] = middle[block]


def call(kernel, name, outs, *args, scratch=()):
    return pl.pallas_call(
        kernel,
        out_shape=outs,
        in_specs=[VMEM] * len(args),
        out_specs=jax.tree.map(lambda _: VMEM, outs),
        scratch_shapes=scratch,
        compiler_params=PARAMS,
        name=name,
    )(*args)


def swaps(count, first):
    pairs = [(i % count, (i + 1) % count) for i in range(first, count, 2)]
    return pairs + [(target, source) for source, target in pairs]


def exchange(near, far):
    radial_size = lax.axis_size("gx")
    return lax.ppermute(near, "gx", swaps(radial_size, 0)), lax.ppermute(far, "gx", swaps(radial_size, 1))


def across(values):
    return lax.all_to_all(values, "gy", 0, 0, tiled=True)


def on_device(state, shifts, fracs, offsets, kappa):
    whole = shape(BLOCKS, ROWS, LANES)
    side = shape(BLOCKS, SIDE_ROWS, LANES)
    message = shape(BLOCKS + 1, SIDE_ROWS, LANES)
    offsets = offsets[None]
    kappa = kappa[None]
    values = across(call(pack_kernel, "pack", whole, state))
    edges, near, far = call(
        advect_edges_kernel,
        "advect_edges",
        (shape(BLOCKS, 2 * SIDE_ROWS, LANES), message, message),
        shifts,
        fracs,
        values,
    )
    halos = exchange(near, far)
    offsets, coefs, back, partial, beyond, unfinished, middle = call(
        inner_kernel,
        "inner",
        (
            jax.ShapeDtypeStruct(offsets.shape, offsets.dtype),
            shape(COEFS, 8, LANES),
            shape(HALF_VARS * NZ, HALF_VARS * NZ),
            side,
            side,
            side,
            shape(BLOCKS, 4 * COL_ROWS, LANES),
        ),
        offsets,
        kappa,
        shifts,
        fracs,
        values,
        edges,
        scratch=[pltpu.VMEM((BLOCKS, ROWS, LANES), F32)] * 2,
    )
    values = call(
        outer_kernel,
        "outer",
        whole,
        offsets,
        coefs,
        shifts,
        fracs,
        edges,
        partial,
        beyond,
        unfinished,
        middle,
        *halos,
        scratch=[pltpu.VMEM((BLOCKS, SIDE_ROWS, LANES), F32)] * 4,
    )
    return call(unpack_kernel, "unpack", shape(VARS, COLS, NZ, LANES), back, across(values))


def solution(mesh):
    placed = (P(None, "gx", None, "gy"), P(None, "gx"), P(None, "gx"), P(), P())
    return jax.shard_map(
        on_device, mesh=mesh, in_specs=placed, out_specs=P(None, "gx", None, "gy"), check_vma=False
    )
```

```python
import math
import jax
import jax.numpy as jnp
from jax import lax
from jax.experimental import pallas as pl
from jax.experimental.pallas import tpu as pltpu
from jax.sharding import PartitionSpec as P

spin_gain = 0.2
spin_drag = 0.05
tidal_gain = 0.3

LANES = 128
BLOCKS = 16
COLS = 8
HALF_VARS = 4
MODES = 4
COL_ROWS = HALF_VARS * MODES
ROWS = COLS * COL_ROWS
HALVES = 2
MODE_BLOCKS = 8
NZ = MODES * MODE_BLOCKS
VARS = HALVES * HALF_VARS
LAST = COLS - 1
SIDE_ROWS = 2 * COL_ROWS
CENTERS = 4 + COLS
GHOST_TIDES = CENTERS + 2
COEFS = GHOST_TIDES + 2

F32 = jnp.float32
VMEM = pl.BlockSpec(memory_space=pltpu.VMEM)
PARAMS = pltpu.CompilerParams(vmem_limit_bytes=28 * 1024 * 1024)


def shape(*dims):
    return jax.ShapeDtypeStruct(dims, F32)


def lane_index():
    return lax.broadcasted_iota(jnp.int32, (8, LANES), 1)


def row_index():
    return lax.broadcasted_iota(jnp.int32, (8, LANES), 0)


def rotated(block, earlier, amount, lanes):
    joined = jnp.where(lanes < LANES - amount, block, earlier)
    return pltpu.roll(joined, amount & (LANES - 1), 1)


def cosine(angle, mode):
    size = jnp.where(mode == 0, (1.0 / NZ) ** 0.5, (2.0 / NZ) ** 0.5)
    return size * jnp.cos((angle & (4 * NZ - 1)).astype(F32) * (math.pi / (2 * NZ)))


def to_modes(transposed):
    dims = (HALF_VARS * NZ, HALF_VARS * NZ)
    row = lax.broadcasted_iota(jnp.int32, dims, 1 if transposed else 0)
    column = lax.broadcasted_iota(jnp.int32, dims, 0 if transposed else 1)
    mode = (row // COL_ROWS) * MODES + row % MODES
    level = column % NZ
    same = (row // MODES) % HALF_VARS == column // NZ
    return jnp.where(same, cosine((2 * level + 1) * mode, mode), 0.0)


def exact_dot(left, right):
    return lax.dot(left, right, precision=lax.Precision.HIGHEST, preferred_element_type=F32)


def pack_kernel(state, out):
    basis = to_modes(False)
    for half in range(HALVES):
        for col in range(COLS):
            levels = jnp.concatenate([state[half * HALF_VARS + var, col] for var in range(HALF_VARS)], axis=0)
            modes = exact_dot(basis, levels)
            for block in range(MODE_BLOCKS):
                out[half * MODE_BLOCKS + block, col * COL_ROWS : (col + 1) * COL_ROWS, :] = modes[
                    block * COL_ROWS : (block + 1) * COL_ROWS
                ]


def unpack_kernel(back, packed, out):
    basis = back[...]
    for half in range(HALVES):
        for col in range(COLS):
            modes = jnp.concatenate(
                [
                    packed[half * MODE_BLOCKS + block, col * COL_ROWS : (col + 1) * COL_ROWS, :]
                    for block in range(MODE_BLOCKS)
                ],
                axis=0,
            )
            levels = exact_dot(basis, modes)
            for var in range(HALF_VARS):
                out[half * HALF_VARS + var, col] = levels[var * NZ : (var + 1) * NZ]


def move(values, block, rows, turn, weight):
    source = (block - turn // LANES) & (BLOCKS - 1)
    before = (source - 1) & (BLOCKS - 1)
    rest = turn & (LANES - 1)
    lanes = lane_index()
    here = values[source, rows, :]
    earlier = values[before, rows, :]
    nearer = rotated(here, earlier, rest, lanes)
    farther = rotated(here, earlier, rest + 1, lanes)
    return (1.0 - weight) * nearer + weight * farther


def is_even(place):
    return (place[0] & 1) == 0


def turned(values, block, rows, turn):
    here = (block - turn // LANES) & (BLOCKS - 1)
    before = (here - 1) & (BLOCKS - 1)
    return rotated(values[here, rows, :], values[before, rows, :], turn & (LANES - 1), lane_index())


def where_am_i():
    around = lax.axis_index("gy")
    return lax.axis_index("gx"), around // MODE_BLOCKS, around % MODE_BLOCKS, lax.axis_size("gx")


def prepare(place, kappa, coefs):
    radial, half, vertical = place[0], place[1], place[2]
    first_half = half == 0
    row = row_index()
    upper_rows = row >= MODES
    mode = vertical * MODES + (row & (MODES - 1))
    own = 2.0 * jnp.cos(mode.astype(F32) * (math.pi / NZ)) - 6.0
    for pair in range(2):
        lower, upper = [
            jnp.where(first_half, kappa[0, 2 * pair + var], kappa[0, HALF_VARS + 2 * pair + var]) for var in range(2)
        ]
        rate = jnp.where(upper_rows, upper, lower)
        coefs[pair] = rate
        coefs[CENTERS + pair] = 1.0 + rate * own
    coupled = jnp.where(first_half, 1.0, 0.0)
    coefs[2] = jnp.where(upper_rows, spin_gain * coupled, 0.0)
    coefs[3] = jnp.where(upper_rows, 0.0, -spin_drag * coupled)
    total = place[3] * COLS
    columns = [(4 + col, radial * COLS + col) for col in range(COLS)]
    columns.append((GHOST_TIDES, jnp.where(radial == 0, total - 1, radial * COLS - 1)))
    columns.append((GHOST_TIDES + 1, jnp.where(radial == place[3] - 1, 0, radial * COLS + COLS)))
    for slot, column in columns:
        position = (column.astype(F32) + 0.5) / float(total) - 0.5
        coefs[slot] = jnp.where(upper_rows, tidal_gain * position * coupled, 0.0)


def sourced(mixed, coefs, tide):
    swapped = [pltpu.roll(part, 4, 0) for part in mixed]
    return mixed[0] + coefs[2] * swapped[1] + tide * swapped[0], mixed[1] + coefs[3] * swapped[0]


def around(values, block, rows):
    lanes = lane_index()
    value = values[block, rows, :]
    after = values[(block + 1) % BLOCKS, rows, :]
    before = values[(block - 1) % BLOCKS, rows, :]
    prior = pltpu.roll(jnp.where(lanes < LANES - 1, value, before), 1, 1)
    following = pltpu.roll(jnp.where(lanes >= 1, value, after), LANES - 1, 1)
    return prior + following


def tiles(start):
    return [pl.ds(start + pair * 8, 8) for pair in range(2)]


def interior(coefs, adv, block, col, low, high):
    mixed = []
    for pair, rows in enumerate(tiles(col * COL_ROWS)):
        beside = [
            adv[block, pl.ds((col + side) * COL_ROWS + pair * 8, 8), :]
            for side in (-1, 1)
            if low <= col + side <= high
        ]
        total = sum(beside[1:], beside[0]) + around(adv, block, rows)
        mixed.append(coefs[CENTERS + pair] * adv[block, rows, :] + coefs[pair] * total)
    return sourced(mixed, coefs, coefs[4 + col])


def side_of(place, crosses):
    even = is_even(place)
    return jnp.where(even, 0, 1) if crosses else jnp.where(even, 1, 0)


def edge_column(side, depth):
    return jnp.where(side == 0, depth, LAST - depth)


def advect_side(crosses, shifts, fracs, values, message):
    side = side_of(where_am_i(), crosses)

    def pick(table, step, depth):
        return jnp.where(side == 0, table[step, depth], table[step, LAST - depth])

    for depth in range(2):
        turn, weight = pick(shifts, 0, depth), pick(fracs, 0, depth)
        start = edge_column(side, depth) * COL_ROWS
        for block in range(BLOCKS):
            for pair in range(2):
                rows = pl.ds(pl.multiple_of(start + pair * 8, 8), 8)
                message[block, pl.ds(depth * COL_ROWS + pair * 8, 8), :] = move(values, block, rows, turn, weight)
    lanes = lane_index()
    turn, weight = pick(shifts, 1, 0).astype(F32), pick(fracs, 1, 0)
    message[BLOCKS] = jnp.zeros((SIDE_ROWS, LANES), F32)
    message[BLOCKS, pl.ds(0, 8), :] = jnp.where(lanes == 0, turn, jnp.where(lanes == 1, weight, 0.0))


def advect_far_kernel(shifts, fracs, values, message):
    advect_side(True, shifts[...], fracs[...], values, message)


def inner_kernel(offsets, kappa, shifts, fracs, values, far, near, offsets_out, coefs, back, partial, beyond, unfinished,
                 middle, adv, current):
    offsets_out[...] = offsets[...]
    back[...] = to_modes(True)
    place = where_am_i()
    prepare(place, kappa[...], coefs)
    shifts = shifts[...]
    fracs = fracs[...]
    advect_side(False, shifts, fracs, values, near)
    for block in range(BLOCKS):
        for message, crosses in ((near, False), (far, True)):
            side = side_of(place, crosses)
            for depth in range(2):
                start = pl.multiple_of(edge_column(side, depth) * COL_ROWS, COL_ROWS)
                adv[block, pl.ds(start, COL_ROWS), :] = message[block, pl.ds(depth * COL_ROWS, COL_ROWS), :]
        for col in range(2, LAST - 1):
            for rows in tiles(col * COL_ROWS):
                adv[block, rows, :] = move(values, block, rows, shifts[0, col], fracs[0, col])
    for block in range(BLOCKS):
        for col in range(COLS):
            for rows, result in zip(tiles(col * COL_ROWS), interior(coefs, adv, block, col, 0, LAST)):
                current[block, rows, :] = result
        partial[block, pl.ds(0, COL_ROWS), :] = current[block, pl.ds(0, COL_ROWS), :]
        partial[block, pl.ds(COL_ROWS, COL_ROWS), :] = current[block, pl.ds(LAST * COL_ROWS, COL_ROWS), :]
    for block in range(BLOCKS):
        for col in range(1, LAST):
            for rows in tiles(col * COL_ROWS):
                adv[block, rows, :] = move(current, block, rows, shifts[1, col], fracs[1, col])
    for block in range(BLOCKS):
        for slot, col in enumerate((1, LAST - 1)):
            beyond[block, pl.ds(slot * COL_ROWS, COL_ROWS), :] = adv[block, pl.ds(col * COL_ROWS, COL_ROWS), :]
        for col in range(1, LAST):
            for pair, result in enumerate(interior(coefs, adv, block, col, 1, LAST - 1)):
                if col == 1:
                    unfinished[block, pl.ds(pair * 8, 8), :] = result
                elif col == LAST - 1:
                    unfinished[block, pl.ds(COL_ROWS + pair * 8, 8), :] = result
                else:
                    middle[block, pl.ds((col - 2) * COL_ROWS + pair * 8, 8), :] = result


def outer_kernel(offsets, coefs, shifts, fracs, near_sent, far_sent, partial, beyond, unfinished, middle, near, far, out,
                 own, ghost, own_moved, ghost_moved):
    place = where_am_i()
    radial, radial_size = place[0], place[3]
    shifts = shifts[...]
    fracs = fracs[...]
    offsets = offsets[...]
    signed = jnp.where(radial == 0, 1, jnp.where(radial == radial_size - 1, -1, 0))
    total_y = BLOCKS * LANES

    def side_tiles(side, base=0):
        return [pl.ds(pl.multiple_of(base + side * COL_ROWS + pair * 8, 8), 8) for pair in range(2)]

    for index, (message, sent) in enumerate(((near, near_sent), (far, far_sent))):
        crosses = index == 1
        side = side_of(place, crosses)
        slots = tiles(index * COL_ROWS)
        own_tide = coefs[4 + LAST * side]
        ghost_tide = coefs[GHOST_TIDES + side]
        next_tide = coefs[5 + (LAST - 2) * side]
        mine = side_tiles(side)
        scalars = message[BLOCKS, pl.ds(0, 8), :]
        ghost_turn = scalars.astype(jnp.int32)[0, 0]
        ghost_weight = scalars[0, 1]
        own_turn = jnp.where(side == 0, shifts[1, 0], shifts[1, LAST])
        own_weight = jnp.where(side == 0, fracs[1, 0], fracs[1, LAST])

        first_turn = (signed * offsets[0, 0]) & (total_y - 1)
        back_turn = (-signed * offsets[0, 0]) & (total_y - 1)
        for block in range(BLOCKS):
            arrived = []
            mixed = []
            for pair, rows in enumerate(tiles(0)):
                value = message[block, rows, :]
                if crosses:
                    incoming = turned(message, block, rows, first_turn)
                    outgoing = turned(sent, block, rows, back_turn)
                else:
                    incoming = value
                    outgoing = sent[block, rows, :]
                arrived.append(coefs[pair] * incoming)
                other = message[block, tiles(COL_ROWS)[pair], :]
                total = (other + outgoing) + around(message, block, rows)
                mixed.append(coefs[CENTERS + pair] * value + coefs[pair] * total)
            for pair, extra in enumerate(sourced(arrived, coefs, own_tide)):
                own[block, slots[pair], :] = partial[block, mine[pair], :] + extra
            for pair, result in enumerate(sourced(mixed, coefs, ghost_tide)):
                ghost[block, slots[pair], :] = result
        for block in range(BLOCKS):
            for rows in slots:
                own_moved[block, rows, :] = move(own, block, rows, own_turn, own_weight)
                ghost_moved[block, rows, :] = move(ghost, block, rows, ghost_turn, ghost_weight)
        last_turn = (signed * offsets[0, 1]) & (total_y - 1)
        own_out = [
            pl.ds(pl.multiple_of(LAST * COL_ROWS * side + pair * 8, 8), 8) for pair in range(2)
        ]
        next_out = [
            pl.ds(pl.multiple_of(COL_ROWS + (LAST - 2) * COL_ROWS * side + pair * 8, 8), 8) for pair in range(2)
        ]
        for block in range(BLOCKS):
            mixed = []
            arrived = []
            for pair, rows in enumerate(slots):
                value = own_moved[block, rows, :]
                if crosses:
                    incoming = turned(ghost_moved, block, rows, last_turn)
                else:
                    incoming = ghost_moved[block, rows, :]
                total = (incoming + beyond[block, mine[pair], :]) + around(own_moved, block, rows)
                mixed.append(coefs[CENTERS + pair] * value + coefs[pair] * total)
                arrived.append(coefs[pair] * value)
            for pair, result in enumerate(sourced(mixed, coefs, own_tide)):
                out[block, own_out[pair], :] = result
            for pair, extra in enumerate(sourced(arrived, coefs, next_tide)):
                out[block, next_out[pair], :] = unfinished[block, mine[pair], :] + extra
    for block in range(BLOCKS):
        out[block, pl.ds(SIDE_ROWS, 4 * COL_ROWS), :] = middle[block]


def call(kernel, name, outs, *args, scratch=()):
    return pl.pallas_call(
        kernel,
        out_shape=outs,
        in_specs=[VMEM] * len(args),
        out_specs=jax.tree.map(lambda _: VMEM, outs),
        scratch_shapes=scratch,
        compiler_params=PARAMS,
        name=name,
    )(*args)


def swaps(count, first):
    pairs = [(i % count, (i + 1) % count) for i in range(first, count, 2)]
    return pairs + [(target, source) for source, target in pairs]


def across(values):
    return lax.all_to_all(values, "gy", 0, 0, tiled=True)


def on_device(state, shifts, fracs, offsets, kappa):
    whole = shape(BLOCKS, ROWS, LANES)
    side = shape(BLOCKS, SIDE_ROWS, LANES)
    offsets = offsets[None]
    kappa = kappa[None]
    values = across(call(pack_kernel, "pack", whole, state))
    message = shape(BLOCKS + 1, SIDE_ROWS, LANES)
    radial_size = lax.axis_size("gx")
    far_sent = call(advect_far_kernel, "advect_far", message, shifts, fracs, values)
    far = lax.ppermute(far_sent, "gx", swaps(radial_size, 1))
    near_sent, offsets, coefs, back, partial, beyond, unfinished, middle = call(
        inner_kernel,
        "inner",
        (
            message,
            jax.ShapeDtypeStruct(offsets.shape, offsets.dtype),
            shape(COEFS, 8, LANES),
            shape(HALF_VARS * NZ, HALF_VARS * NZ),
            side,
            side,
            side,
            shape(BLOCKS, 4 * COL_ROWS, LANES),
        ),
        offsets,
        kappa,
        shifts,
        fracs,
        values,
        far_sent,
        scratch=[pltpu.VMEM((BLOCKS, ROWS, LANES), F32)] * 2,
    )
    near = lax.ppermute(near_sent, "gx", swaps(radial_size, 0))
    values = call(
        outer_kernel,
        "outer",
        whole,
        offsets,
        coefs,
        shifts,
        fracs,
        near_sent,
        far_sent,
        partial,
        beyond,
        unfinished,
        middle,
        near,
        far,
        scratch=[pltpu.VMEM((BLOCKS, SIDE_ROWS, LANES), F32)] * 4,
    )
    return call(unpack_kernel, "unpack", shape(VARS, COLS, NZ, LANES), back, across(values))


def solution(mesh):
    placed = (P(None, "gx", None, "gy"), P(None, "gx"), P(None, "gx"), P(), P())
    return jax.shard_map(
        on_device, mesh=mesh, in_specs=placed, out_specs=P(None, "gx", None, "gy"), check_vma=False
    )
```

```python
import math
import jax
import jax.numpy as jnp
from jax import lax
from jax.experimental import pallas as pl
from jax.experimental.pallas import tpu as pltpu
from jax.sharding import PartitionSpec as P

spin_gain = 0.2
spin_drag = 0.05
tidal_gain = 0.3

LANES = 128
BLOCKS = 16
COLS = 8
HALF_VARS = 4
MODES = 4
COL_ROWS = HALF_VARS * MODES
ROWS = COLS * COL_ROWS
HALVES = 2
MODE_BLOCKS = 8
NZ = MODES * MODE_BLOCKS
VARS = HALVES * HALF_VARS
LAST = COLS - 1
SIDE_ROWS = 2 * COL_ROWS
CENTERS = 4 + COLS
GHOST_TIDES = CENTERS + 2
COEFS = GHOST_TIDES + 2

F32 = jnp.float32
VMEM = pl.BlockSpec(memory_space=pltpu.VMEM)
PARAMS = pltpu.CompilerParams(vmem_limit_bytes=28 * 1024 * 1024)


def shape(*dims):
    return jax.ShapeDtypeStruct(dims, F32)


def lane_index():
    return lax.broadcasted_iota(jnp.int32, (8, LANES), 1)


def row_index():
    return lax.broadcasted_iota(jnp.int32, (8, LANES), 0)


def rotated(block, earlier, amount, lanes):
    joined = jnp.where(lanes < LANES - amount, block, earlier)
    return pltpu.roll(joined, amount & (LANES - 1), 1)


def cosine(angle, mode):
    size = jnp.where(mode == 0, (1.0 / NZ) ** 0.5, (2.0 / NZ) ** 0.5)
    return size * jnp.cos((angle & (4 * NZ - 1)).astype(F32) * (math.pi / (2 * NZ)))


def to_modes(transposed):
    dims = (HALF_VARS * NZ, HALF_VARS * NZ)
    row = lax.broadcasted_iota(jnp.int32, dims, 1 if transposed else 0)
    column = lax.broadcasted_iota(jnp.int32, dims, 0 if transposed else 1)
    mode = (row // COL_ROWS) * MODES + row % MODES
    level = column % NZ
    same = (row // MODES) % HALF_VARS == column // NZ
    return jnp.where(same, cosine((2 * level + 1) * mode, mode), 0.0)


def exact_dot(left, right):
    return lax.dot(left, right, precision=lax.Precision.HIGHEST, preferred_element_type=F32)


def pack_kernel(state, out):
    basis = to_modes(False)
    for half in range(HALVES):
        for col in range(COLS):
            levels = jnp.concatenate([state[half * HALF_VARS + var, col] for var in range(HALF_VARS)], axis=0)
            modes = exact_dot(basis, levels)
            for block in range(MODE_BLOCKS):
                out[half * MODE_BLOCKS + block, col * COL_ROWS : (col + 1) * COL_ROWS, :] = modes[
                    block * COL_ROWS : (block + 1) * COL_ROWS
                ]


def unpack_kernel(back, packed, out, held, left):
    basis = back[...]
    copies = []
    for half in range(HALVES):
        for col in range(COLS):
            modes = jnp.concatenate(
                [
                    packed[half * MODE_BLOCKS + block, col * COL_ROWS : (col + 1) * COL_ROWS, :]
                    for block in range(MODE_BLOCKS)
                ],
                axis=0,
            )
            levels = exact_dot(basis, modes)
            for var in range(HALF_VARS):
                held[half * HALF_VARS + var, col] = levels[var * NZ : (var + 1) * NZ]
            part = pl.ds(half * HALF_VARS, HALF_VARS)
            copy = pltpu.make_async_copy(held.at[part, col], out.at[part, col], left.at[half * COLS + col])
            copy.start()
            copies.append(copy)
    for copy in copies:
        copy.wait()


def move(values, block, rows, turn, weight):
    source = (block - turn // LANES) & (BLOCKS - 1)
    before = (source - 1) & (BLOCKS - 1)
    rest = turn & (LANES - 1)
    lanes = lane_index()
    here = values[source, rows, :]
    earlier = values[before, rows, :]
    nearer = rotated(here, earlier, rest, lanes)
    farther = rotated(here, earlier, rest + 1, lanes)
    return (1.0 - weight) * nearer + weight * farther


def is_even(place):
    return (place[0] & 1) == 0


def turned(values, block, rows, turn):
    here = (block - turn // LANES) & (BLOCKS - 1)
    before = (here - 1) & (BLOCKS - 1)
    return rotated(values[here, rows, :], values[before, rows, :], turn & (LANES - 1), lane_index())


def where_am_i():
    around = lax.axis_index("gy")
    return lax.axis_index("gx"), around // MODE_BLOCKS, around % MODE_BLOCKS, lax.axis_size("gx")


def prepare(place, kappa, coefs):
    radial, half, vertical = place[0], place[1], place[2]
    first_half = half == 0
    row = row_index()
    upper_rows = row >= MODES
    mode = vertical * MODES + (row & (MODES - 1))
    own = 2.0 * jnp.cos(mode.astype(F32) * (math.pi / NZ)) - 6.0
    for pair in range(2):
        lower, upper = [
            jnp.where(first_half, kappa[0, 2 * pair + var], kappa[0, HALF_VARS + 2 * pair + var]) for var in range(2)
        ]
        rate = jnp.where(upper_rows, upper, lower)
        coefs[pair] = rate
        coefs[CENTERS + pair] = 1.0 + rate * own
    coupled = jnp.where(first_half, 1.0, 0.0)
    coefs[2] = jnp.where(upper_rows, spin_gain * coupled, 0.0)
    coefs[3] = jnp.where(upper_rows, 0.0, -spin_drag * coupled)
    total = place[3] * COLS
    columns = [(4 + col, radial * COLS + col) for col in range(COLS)]
    columns.append((GHOST_TIDES, jnp.where(radial == 0, total - 1, radial * COLS - 1)))
    columns.append((GHOST_TIDES + 1, jnp.where(radial == place[3] - 1, 0, radial * COLS + COLS)))
    for slot, column in columns:
        position = (column.astype(F32) + 0.5) / float(total) - 0.5
        coefs[slot] = jnp.where(upper_rows, tidal_gain * position * coupled, 0.0)


def sourced(mixed, coefs, tide):
    swapped = [pltpu.roll(part, 4, 0) for part in mixed]
    return mixed[0] + coefs[2] * swapped[1] + tide * swapped[0], mixed[1] + coefs[3] * swapped[0]


def around(values, block, rows):
    lanes = lane_index()
    value = values[block, rows, :]
    after = values[(block + 1) % BLOCKS, rows, :]
    before = values[(block - 1) % BLOCKS, rows, :]
    prior = pltpu.roll(jnp.where(lanes < LANES - 1, value, before), 1, 1)
    following = pltpu.roll(jnp.where(lanes >= 1, value, after), LANES - 1, 1)
    return prior + following


def tiles(start):
    return [pl.ds(start + pair * 8, 8) for pair in range(2)]


def interior(coefs, adv, block, col, low, high):
    mixed = []
    for pair, rows in enumerate(tiles(col * COL_ROWS)):
        beside = [
            adv[block, pl.ds((col + side) * COL_ROWS + pair * 8, 8), :]
            for side in (-1, 1)
            if low <= col + side <= high
        ]
        total = sum(beside[1:], beside[0]) + around(adv, block, rows)
        mixed.append(coefs[CENTERS + pair] * adv[block, rows, :] + coefs[pair] * total)
    return sourced(mixed, coefs, coefs[4 + col])


def side_of(place, crosses):
    even = is_even(place)
    return jnp.where(even, 0, 1) if crosses else jnp.where(even, 1, 0)


def edge_column(side, depth):
    return jnp.where(side == 0, depth, LAST - depth)


def advect_side(crosses, shifts, fracs, values, message):
    side = side_of(where_am_i(), crosses)

    def pick(table, step, depth):
        return jnp.where(side == 0, table[step, depth], table[step, LAST - depth])

    for depth in range(2):
        turn, weight = pick(shifts, 0, depth), pick(fracs, 0, depth)
        start = edge_column(side, depth) * COL_ROWS
        for block in range(BLOCKS):
            for pair in range(2):
                rows = pl.ds(pl.multiple_of(start + pair * 8, 8), 8)
                message[block, pl.ds(depth * COL_ROWS + pair * 8, 8), :] = move(values, block, rows, turn, weight)
    lanes = lane_index()
    turn, weight = pick(shifts, 1, 0).astype(F32), pick(fracs, 1, 0)
    message[BLOCKS] = jnp.zeros((SIDE_ROWS, LANES), F32)
    message[BLOCKS, pl.ds(0, 8), :] = jnp.where(lanes == 0, turn, jnp.where(lanes == 1, weight, 0.0))


def advect_far_kernel(shifts, fracs, values, message):
    advect_side(True, shifts[...], fracs[...], values, message)


def inner_kernel(offsets, kappa, shifts, fracs, values, far, near, offsets_out, coefs, back, partial, beyond, unfinished,
                 middle, adv, current):
    offsets_out[...] = offsets[...]
    back[...] = to_modes(True)
    place = where_am_i()
    prepare(place, kappa[...], coefs)
    shifts = shifts[...]
    fracs = fracs[...]
    advect_side(False, shifts, fracs, values, near)
    for block in range(BLOCKS):
        for message, crosses in ((near, False), (far, True)):
            side = side_of(place, crosses)
            for depth in range(2):
                start = pl.multiple_of(edge_column(side, depth) * COL_ROWS, COL_ROWS)
                adv[block, pl.ds(start, COL_ROWS), :] = message[block, pl.ds(depth * COL_ROWS, COL_ROWS), :]
        for col in range(2, LAST - 1):
            for rows in tiles(col * COL_ROWS):
                adv[block, rows, :] = move(values, block, rows, shifts[0, col], fracs[0, col])
    for block in range(BLOCKS):
        for col in range(COLS):
            for rows, result in zip(tiles(col * COL_ROWS), interior(coefs, adv, block, col, 0, LAST)):
                current[block, rows, :] = result
        partial[block, pl.ds(0, COL_ROWS), :] = current[block, pl.ds(0, COL_ROWS), :]
        partial[block, pl.ds(COL_ROWS, COL_ROWS), :] = current[block, pl.ds(LAST * COL_ROWS, COL_ROWS), :]
    for block in range(BLOCKS):
        for col in range(1, LAST):
            for rows in tiles(col * COL_ROWS):
                adv[block, rows, :] = move(current, block, rows, shifts[1, col], fracs[1, col])
    for block in range(BLOCKS):
        for slot, col in enumerate((1, LAST - 1)):
            beyond[block, pl.ds(slot * COL_ROWS, COL_ROWS), :] = adv[block, pl.ds(col * COL_ROWS, COL_ROWS), :]
        for col in range(1, LAST):
            for pair, result in enumerate(interior(coefs, adv, block, col, 1, LAST - 1)):
                if col == 1:
                    unfinished[block, pl.ds(pair * 8, 8), :] = result
                elif col == LAST - 1:
                    unfinished[block, pl.ds(COL_ROWS + pair * 8, 8), :] = result
                else:
                    middle[block, pl.ds((col - 2) * COL_ROWS + pair * 8, 8), :] = result


def outer_kernel(offsets, coefs, shifts, fracs, near_sent, far_sent, partial, beyond, unfinished, middle, near, far, out,
                 own, ghost, own_moved, ghost_moved):
    place = where_am_i()
    radial, radial_size = place[0], place[3]
    shifts = shifts[...]
    fracs = fracs[...]
    offsets = offsets[...]
    signed = jnp.where(radial == 0, 1, jnp.where(radial == radial_size - 1, -1, 0))
    total_y = BLOCKS * LANES

    def side_tiles(side, base=0):
        return [pl.ds(pl.multiple_of(base + side * COL_ROWS + pair * 8, 8), 8) for pair in range(2)]

    for index, (message, sent) in enumerate(((near, near_sent), (far, far_sent))):
        crosses = index == 1
        side = side_of(place, crosses)
        slots = tiles(index * COL_ROWS)
        own_tide = coefs[4 + LAST * side]
        ghost_tide = coefs[GHOST_TIDES + side]
        next_tide = coefs[5 + (LAST - 2) * side]
        mine = side_tiles(side)
        scalars = message[BLOCKS, pl.ds(0, 8), :]
        ghost_turn = scalars.astype(jnp.int32)[0, 0]
        ghost_weight = scalars[0, 1]
        own_turn = jnp.where(side == 0, shifts[1, 0], shifts[1, LAST])
        own_weight = jnp.where(side == 0, fracs[1, 0], fracs[1, LAST])

        first_turn = (signed * offsets[0, 0]) & (total_y - 1)
        back_turn = (-signed * offsets[0, 0]) & (total_y - 1)
        for block in range(BLOCKS):
            arrived = []
            mixed = []
            for pair, rows in enumerate(tiles(0)):
                value = message[block, rows, :]
                if crosses:
                    incoming = turned(message, block, rows, first_turn)
                    outgoing = turned(sent, block, rows, back_turn)
                else:
                    incoming = value
                    outgoing = sent[block, rows, :]
                arrived.append(coefs[pair] * incoming)
                other = message[block, tiles(COL_ROWS)[pair], :]
                total = (other + outgoing) + around(message, block, rows)
                mixed.append(coefs[CENTERS + pair] * value + coefs[pair] * total)
            for pair, extra in enumerate(sourced(arrived, coefs, own_tide)):
                own[block, slots[pair], :] = partial[block, mine[pair], :] + extra
            for pair, result in enumerate(sourced(mixed, coefs, ghost_tide)):
                ghost[block, slots[pair], :] = result
        for block in range(BLOCKS):
            for rows in slots:
                own_moved[block, rows, :] = move(own, block, rows, own_turn, own_weight)
                ghost_moved[block, rows, :] = move(ghost, block, rows, ghost_turn, ghost_weight)
        last_turn = (signed * offsets[0, 1]) & (total_y - 1)
        own_out = [
            pl.ds(pl.multiple_of(LAST * COL_ROWS * side + pair * 8, 8), 8) for pair in range(2)
        ]
        next_out = [
            pl.ds(pl.multiple_of(COL_ROWS + (LAST - 2) * COL_ROWS * side + pair * 8, 8), 8) for pair in range(2)
        ]
        for block in range(BLOCKS):
            mixed = []
            arrived = []
            for pair, rows in enumerate(slots):
                value = own_moved[block, rows, :]
                if crosses:
                    incoming = turned(ghost_moved, block, rows, last_turn)
                else:
                    incoming = ghost_moved[block, rows, :]
                total = (incoming + beyond[block, mine[pair], :]) + around(own_moved, block, rows)
                mixed.append(coefs[CENTERS + pair] * value + coefs[pair] * total)
                arrived.append(coefs[pair] * value)
            for pair, result in enumerate(sourced(mixed, coefs, own_tide)):
                out[block, own_out[pair], :] = result
            for pair, extra in enumerate(sourced(arrived, coefs, next_tide)):
                out[block, next_out[pair], :] = unfinished[block, mine[pair], :] + extra
    for block in range(BLOCKS):
        out[block, pl.ds(SIDE_ROWS, 4 * COL_ROWS), :] = middle[block]


def call(kernel, name, outs, *args, scratch=()):
    return pl.pallas_call(
        kernel,
        out_shape=outs,
        in_specs=[VMEM] * len(args),
        out_specs=jax.tree.map(lambda _: VMEM, outs),
        scratch_shapes=scratch,
        compiler_params=PARAMS,
        name=name,
    )(*args)


def unpack(back, values):
    dims = (VARS, COLS, NZ, LANES)
    return pl.pallas_call(
        unpack_kernel,
        out_shape=shape(*dims),
        in_specs=[VMEM, VMEM],
        out_specs=pl.BlockSpec(memory_space=pl.ANY),
        scratch_shapes=[pltpu.VMEM(dims, F32), pltpu.SemaphoreType.DMA((HALVES * COLS,))],
        compiler_params=PARAMS,
        name="unpack",
    )(back, values)


def swaps(count, first):
    pairs = [(i % count, (i + 1) % count) for i in range(first, count, 2)]
    return pairs + [(target, source) for source, target in pairs]


def across(values):
    return lax.all_to_all(values, "gy", 0, 0, tiled=True)


def on_device(state, shifts, fracs, offsets, kappa):
    whole = shape(BLOCKS, ROWS, LANES)
    side = shape(BLOCKS, SIDE_ROWS, LANES)
    offsets = offsets[None]
    kappa = kappa[None]
    values = across(call(pack_kernel, "pack", whole, state))
    message = shape(BLOCKS + 1, SIDE_ROWS, LANES)
    radial_size = lax.axis_size("gx")
    far_sent = call(advect_far_kernel, "advect_far", message, shifts, fracs, values)
    far = lax.ppermute(far_sent, "gx", swaps(radial_size, 1))
    near_sent, offsets, coefs, back, partial, beyond, unfinished, middle = call(
        inner_kernel,
        "inner",
        (
            message,
            jax.ShapeDtypeStruct(offsets.shape, offsets.dtype),
            shape(COEFS, 8, LANES),
            shape(HALF_VARS * NZ, HALF_VARS * NZ),
            side,
            side,
            side,
            shape(BLOCKS, 4 * COL_ROWS, LANES),
        ),
        offsets,
        kappa,
        shifts,
        fracs,
        values,
        far_sent,
        scratch=[pltpu.VMEM((BLOCKS, ROWS, LANES), F32)] * 2,
    )
    near = lax.ppermute(near_sent, "gx", swaps(radial_size, 0))
    values = call(
        outer_kernel,
        "outer",
        whole,
        offsets,
        coefs,
        shifts,
        fracs,
        near_sent,
        far_sent,
        partial,
        beyond,
        unfinished,
        middle,
        near,
        far,
        scratch=[pltpu.VMEM((BLOCKS, SIDE_ROWS, LANES), F32)] * 4,
    )
    return unpack(back, across(values))


def solution(mesh):
    placed = (P(None, "gx", None, "gy"), P(None, "gx"), P(None, "gx"), P(), P())
    return jax.shard_map(
        on_device, mesh=mesh, in_specs=placed, out_specs=P(None, "gx", None, "gy"), check_vma=False
    )
```

```python
import math
import jax
import jax.numpy as jnp
from jax import lax
from jax.experimental import pallas as pl
from jax.experimental.pallas import tpu as pltpu
from jax.sharding import PartitionSpec as P

spin_gain = 0.2
spin_drag = 0.05
tidal_gain = 0.3

LANES = 128
BLOCKS = 16
COLS = 8
HALF_VARS = 4
MODES = 4
COL_ROWS = HALF_VARS * MODES
ROWS = COLS * COL_ROWS
HALVES = 2
MODE_BLOCKS = 8
NZ = MODES * MODE_BLOCKS
VARS = HALVES * HALF_VARS
LAST = COLS - 1
SIDE_ROWS = 2 * COL_ROWS
CENTERS = 4 + COLS
GHOST_TIDES = CENTERS + 2
COEFS = GHOST_TIDES + 2

F32 = jnp.float32
VMEM = pl.BlockSpec(memory_space=pltpu.VMEM)
PARAMS = pltpu.CompilerParams(vmem_limit_bytes=28 * 1024 * 1024)


def shape(*dims):
    return jax.ShapeDtypeStruct(dims, F32)


def lane_index():
    return lax.broadcasted_iota(jnp.int32, (8, LANES), 1)


def row_index():
    return lax.broadcasted_iota(jnp.int32, (8, LANES), 0)


def rotated(block, earlier, amount, lanes):
    joined = jnp.where(lanes < LANES - amount, block, earlier)
    return pltpu.roll(joined, amount & (LANES - 1), 1)


def cosine(angle, mode):
    size = jnp.where(mode == 0, (1.0 / NZ) ** 0.5, (2.0 / NZ) ** 0.5)
    return size * jnp.cos((angle & (4 * NZ - 1)).astype(F32) * (math.pi / (2 * NZ)))


def to_modes(transposed):
    dims = (HALF_VARS * NZ, HALF_VARS * NZ)
    row = lax.broadcasted_iota(jnp.int32, dims, 1 if transposed else 0)
    column = lax.broadcasted_iota(jnp.int32, dims, 0 if transposed else 1)
    mode = (row // COL_ROWS) * MODES + row % MODES
    level = column % NZ
    same = (row // MODES) % HALF_VARS == column // NZ
    return jnp.where(same, cosine((2 * level + 1) * mode, mode), 0.0)


def exact_dot(left, right):
    return lax.dot(left, right, precision=lax.Precision.HIGHEST, preferred_element_type=F32)


def basis_kernel(out):
    out[...] = to_modes(False)


def pack_kernel(forth, state, out):
    basis = forth[...]
    for half in range(HALVES):
        for col in range(COLS):
            levels = jnp.concatenate([state[half * HALF_VARS + var, col] for var in range(HALF_VARS)], axis=0)
            modes = exact_dot(basis, levels)
            for block in range(MODE_BLOCKS):
                out[half * MODE_BLOCKS + block, col * COL_ROWS : (col + 1) * COL_ROWS, :] = modes[
                    block * COL_ROWS : (block + 1) * COL_ROWS
                ]


def unpack_kernel(back, packed, out, held, left):
    basis = back[...]
    copies = []
    for half in range(HALVES):
        for col in range(COLS):
            modes = jnp.concatenate(
                [
                    packed[half * MODE_BLOCKS + block, col * COL_ROWS : (col + 1) * COL_ROWS, :]
                    for block in range(MODE_BLOCKS)
                ],
                axis=0,
            )
            levels = exact_dot(basis, modes)
            for var in range(HALF_VARS):
                held[half * HALF_VARS + var, col] = levels[var * NZ : (var + 1) * NZ]
            part = pl.ds(half * HALF_VARS, HALF_VARS)
            copy = pltpu.make_async_copy(held.at[part, col], out.at[part, col], left.at[half * COLS + col])
            copy.start()
            copies.append(copy)
    for copy in copies:
        copy.wait()


def move(values, block, rows, turn, weight):
    source = (block - turn // LANES) & (BLOCKS - 1)
    before = (source - 1) & (BLOCKS - 1)
    rest = turn & (LANES - 1)
    lanes = lane_index()
    here = values[source, rows, :]
    earlier = values[before, rows, :]
    nearer = rotated(here, earlier, rest, lanes)
    farther = rotated(here, earlier, rest + 1, lanes)
    return (1.0 - weight) * nearer + weight * farther


def is_even(place):
    return (place[0] & 1) == 0


def turned(values, block, rows, turn):
    here = (block - turn // LANES) & (BLOCKS - 1)
    before = (here - 1) & (BLOCKS - 1)
    return rotated(values[here, rows, :], values[before, rows, :], turn & (LANES - 1), lane_index())


def where_am_i():
    around = lax.axis_index("gy")
    return lax.axis_index("gx"), around // MODE_BLOCKS, around % MODE_BLOCKS, lax.axis_size("gx")


def prepare(place, kappa, coefs):
    radial, half, vertical = place[0], place[1], place[2]
    first_half = half == 0
    row = row_index()
    upper_rows = row >= MODES
    mode = vertical * MODES + (row & (MODES - 1))
    own = 2.0 * jnp.cos(mode.astype(F32) * (math.pi / NZ)) - 6.0
    for pair in range(2):
        lower, upper = [
            jnp.where(first_half, kappa[0, 2 * pair + var], kappa[0, HALF_VARS + 2 * pair + var]) for var in range(2)
        ]
        rate = jnp.where(upper_rows, upper, lower)
        coefs[pair] = rate
        coefs[CENTERS + pair] = 1.0 + rate * own
    coupled = jnp.where(first_half, 1.0, 0.0)
    coefs[2] = jnp.where(upper_rows, spin_gain * coupled, 0.0)
    coefs[3] = jnp.where(upper_rows, 0.0, -spin_drag * coupled)
    total = place[3] * COLS
    columns = [(4 + col, radial * COLS + col) for col in range(COLS)]
    columns.append((GHOST_TIDES, jnp.where(radial == 0, total - 1, radial * COLS - 1)))
    columns.append((GHOST_TIDES + 1, jnp.where(radial == place[3] - 1, 0, radial * COLS + COLS)))
    for slot, column in columns:
        position = (column.astype(F32) + 0.5) / float(total) - 0.5
        coefs[slot] = jnp.where(upper_rows, tidal_gain * position * coupled, 0.0)


def sourced(mixed, coefs, tide):
    swapped = [pltpu.roll(part, 4, 0) for part in mixed]
    return mixed[0] + coefs[2] * swapped[1] + tide * swapped[0], mixed[1] + coefs[3] * swapped[0]


def around(values, block, rows):
    lanes = lane_index()
    value = values[block, rows, :]
    after = values[(block + 1) % BLOCKS, rows, :]
    before = values[(block - 1) % BLOCKS, rows, :]
    prior = pltpu.roll(jnp.where(lanes < LANES - 1, value, before), 1, 1)
    following = pltpu.roll(jnp.where(lanes >= 1, value, after), LANES - 1, 1)
    return prior + following


def tiles(start):
    return [pl.ds(start + pair * 8, 8) for pair in range(2)]


def interior(coefs, adv, block, col, low, high):
    mixed = []
    for pair, rows in enumerate(tiles(col * COL_ROWS)):
        beside = [
            adv[block, pl.ds((col + side) * COL_ROWS + pair * 8, 8), :]
            for side in (-1, 1)
            if low <= col + side <= high
        ]
        total = sum(beside[1:], beside[0]) + around(adv, block, rows)
        mixed.append(coefs[CENTERS + pair] * adv[block, rows, :] + coefs[pair] * total)
    return sourced(mixed, coefs, coefs[4 + col])


def side_of(place, crosses):
    even = is_even(place)
    return jnp.where(even, 0, 1) if crosses else jnp.where(even, 1, 0)


def edge_column(side, depth):
    return jnp.where(side == 0, depth, LAST - depth)


def advect_side(crosses, shifts, fracs, values, message):
    side = side_of(where_am_i(), crosses)

    def pick(table, step, depth):
        return jnp.where(side == 0, table[step, depth], table[step, LAST - depth])

    for depth in range(2):
        turn, weight = pick(shifts, 0, depth), pick(fracs, 0, depth)
        start = edge_column(side, depth) * COL_ROWS
        for block in range(BLOCKS):
            for pair in range(2):
                rows = pl.ds(pl.multiple_of(start + pair * 8, 8), 8)
                message[block, pl.ds(depth * COL_ROWS + pair * 8, 8), :] = move(values, block, rows, turn, weight)
    lanes = lane_index()
    turn, weight = pick(shifts, 1, 0).astype(F32), pick(fracs, 1, 0)
    message[BLOCKS] = jnp.zeros((SIDE_ROWS, LANES), F32)
    message[BLOCKS, pl.ds(0, 8), :] = jnp.where(lanes == 0, turn, jnp.where(lanes == 1, weight, 0.0))


def advect_far_kernel(shifts, fracs, values, message):
    advect_side(True, shifts[...], fracs[...], values, message)


def inner_kernel(offsets, kappa, shifts, fracs, values, far, near, offsets_out, coefs, back, partial, beyond, unfinished,
                 middle, adv, current):
    offsets_out[...] = offsets[...]
    back[...] = to_modes(True)
    place = where_am_i()
    prepare(place, kappa[...], coefs)
    shifts = shifts[...]
    fracs = fracs[...]
    advect_side(False, shifts, fracs, values, near)
    for block in range(BLOCKS):
        for message, crosses in ((near, False), (far, True)):
            side = side_of(place, crosses)
            for depth in range(2):
                start = pl.multiple_of(edge_column(side, depth) * COL_ROWS, COL_ROWS)
                adv[block, pl.ds(start, COL_ROWS), :] = message[block, pl.ds(depth * COL_ROWS, COL_ROWS), :]
        for col in range(2, LAST - 1):
            for rows in tiles(col * COL_ROWS):
                adv[block, rows, :] = move(values, block, rows, shifts[0, col], fracs[0, col])
    for block in range(BLOCKS):
        for col in range(COLS):
            for rows, result in zip(tiles(col * COL_ROWS), interior(coefs, adv, block, col, 0, LAST)):
                current[block, rows, :] = result
        partial[block, pl.ds(0, COL_ROWS), :] = current[block, pl.ds(0, COL_ROWS), :]
        partial[block, pl.ds(COL_ROWS, COL_ROWS), :] = current[block, pl.ds(LAST * COL_ROWS, COL_ROWS), :]
    for block in range(BLOCKS):
        for col in range(1, LAST):
            for rows in tiles(col * COL_ROWS):
                adv[block, rows, :] = move(current, block, rows, shifts[1, col], fracs[1, col])
    for block in range(BLOCKS):
        for slot, col in enumerate((1, LAST - 1)):
            beyond[block, pl.ds(slot * COL_ROWS, COL_ROWS), :] = adv[block, pl.ds(col * COL_ROWS, COL_ROWS), :]
        for col in range(1, LAST):
            for pair, result in enumerate(interior(coefs, adv, block, col, 1, LAST - 1)):
                if col == 1:
                    unfinished[block, pl.ds(pair * 8, 8), :] = result
                elif col == LAST - 1:
                    unfinished[block, pl.ds(COL_ROWS + pair * 8, 8), :] = result
                else:
                    middle[block, pl.ds((col - 2) * COL_ROWS + pair * 8, 8), :] = result


def outer_kernel(offsets, coefs, shifts, fracs, near_sent, far_sent, partial, beyond, unfinished, middle, near, far, out,
                 own, ghost, own_moved, ghost_moved):
    place = where_am_i()
    radial, radial_size = place[0], place[3]
    shifts = shifts[...]
    fracs = fracs[...]
    offsets = offsets[...]
    signed = jnp.where(radial == 0, 1, jnp.where(radial == radial_size - 1, -1, 0))
    total_y = BLOCKS * LANES

    def side_tiles(side, base=0):
        return [pl.ds(pl.multiple_of(base + side * COL_ROWS + pair * 8, 8), 8) for pair in range(2)]

    for index, (message, sent) in enumerate(((near, near_sent), (far, far_sent))):
        crosses = index == 1
        side = side_of(place, crosses)
        slots = tiles(index * COL_ROWS)
        own_tide = coefs[4 + LAST * side]
        ghost_tide = coefs[GHOST_TIDES + side]
        next_tide = coefs[5 + (LAST - 2) * side]
        mine = side_tiles(side)
        scalars = message[BLOCKS, pl.ds(0, 8), :]
        ghost_turn = scalars.astype(jnp.int32)[0, 0]
        ghost_weight = scalars[0, 1]
        own_turn = jnp.where(side == 0, shifts[1, 0], shifts[1, LAST])
        own_weight = jnp.where(side == 0, fracs[1, 0], fracs[1, LAST])

        first_turn = (signed * offsets[0, 0]) & (total_y - 1)
        back_turn = (-signed * offsets[0, 0]) & (total_y - 1)
        for block in range(BLOCKS):
            arrived = []
            mixed = []
            for pair, rows in enumerate(tiles(0)):
                value = message[block, rows, :]
                if crosses:
                    incoming = turned(message, block, rows, first_turn)
                    outgoing = turned(sent, block, rows, back_turn)
                else:
                    incoming = value
                    outgoing = sent[block, rows, :]
                arrived.append(coefs[pair] * incoming)
                other = message[block, tiles(COL_ROWS)[pair], :]
                total = (other + outgoing) + around(message, block, rows)
                mixed.append(coefs[CENTERS + pair] * value + coefs[pair] * total)
            for pair, extra in enumerate(sourced(arrived, coefs, own_tide)):
                own[block, slots[pair], :] = partial[block, mine[pair], :] + extra
            for pair, result in enumerate(sourced(mixed, coefs, ghost_tide)):
                ghost[block, slots[pair], :] = result
        for block in range(BLOCKS):
            for rows in slots:
                own_moved[block, rows, :] = move(own, block, rows, own_turn, own_weight)
                ghost_moved[block, rows, :] = move(ghost, block, rows, ghost_turn, ghost_weight)
        last_turn = (signed * offsets[0, 1]) & (total_y - 1)
        own_out = [
            pl.ds(pl.multiple_of(LAST * COL_ROWS * side + pair * 8, 8), 8) for pair in range(2)
        ]
        next_out = [
            pl.ds(pl.multiple_of(COL_ROWS + (LAST - 2) * COL_ROWS * side + pair * 8, 8), 8) for pair in range(2)
        ]
        for block in range(BLOCKS):
            mixed = []
            arrived = []
            for pair, rows in enumerate(slots):
                value = own_moved[block, rows, :]
                if crosses:
                    incoming = turned(ghost_moved, block, rows, last_turn)
                else:
                    incoming = ghost_moved[block, rows, :]
                total = (incoming + beyond[block, mine[pair], :]) + around(own_moved, block, rows)
                mixed.append(coefs[CENTERS + pair] * value + coefs[pair] * total)
                arrived.append(coefs[pair] * value)
            for pair, result in enumerate(sourced(mixed, coefs, own_tide)):
                out[block, own_out[pair], :] = result
            for pair, extra in enumerate(sourced(arrived, coefs, next_tide)):
                out[block, next_out[pair], :] = unfinished[block, mine[pair], :] + extra
    for block in range(BLOCKS):
        out[block, pl.ds(SIDE_ROWS, 4 * COL_ROWS), :] = middle[block]


def call(kernel, name, outs, *args, scratch=()):
    return pl.pallas_call(
        kernel,
        out_shape=outs,
        in_specs=[VMEM] * len(args),
        out_specs=jax.tree.map(lambda _: VMEM, outs),
        scratch_shapes=scratch,
        compiler_params=PARAMS,
        name=name,
    )(*args)


def unpack(back, values):
    dims = (VARS, COLS, NZ, LANES)
    return pl.pallas_call(
        unpack_kernel,
        out_shape=shape(*dims),
        in_specs=[VMEM, VMEM],
        out_specs=pl.BlockSpec(memory_space=pl.ANY),
        scratch_shapes=[pltpu.VMEM(dims, F32), pltpu.SemaphoreType.DMA((HALVES * COLS,))],
        compiler_params=PARAMS,
        name="unpack",
    )(back, values)


def swaps(count, first):
    pairs = [(i % count, (i + 1) % count) for i in range(first, count, 2)]
    return pairs + [(target, source) for source, target in pairs]


def across(values):
    return lax.all_to_all(values, "gy", 0, 0, tiled=True)


def on_device(state, shifts, fracs, offsets, kappa):
    whole = shape(BLOCKS, ROWS, LANES)
    side = shape(BLOCKS, SIDE_ROWS, LANES)
    offsets = offsets[None]
    kappa = kappa[None]
    forth = call(basis_kernel, "basis", shape(HALF_VARS * NZ, HALF_VARS * NZ))
    values = across(call(pack_kernel, "pack", whole, forth, state))
    message = shape(BLOCKS + 1, SIDE_ROWS, LANES)
    radial_size = lax.axis_size("gx")
    far_sent = call(advect_far_kernel, "advect_far", message, shifts, fracs, values)
    far = lax.ppermute(far_sent, "gx", swaps(radial_size, 1))
    near_sent, offsets, coefs, back, partial, beyond, unfinished, middle = call(
        inner_kernel,
        "inner",
        (
            message,
            jax.ShapeDtypeStruct(offsets.shape, offsets.dtype),
            shape(COEFS, 8, LANES),
            shape(HALF_VARS * NZ, HALF_VARS * NZ),
            side,
            side,
            side,
            shape(BLOCKS, 4 * COL_ROWS, LANES),
        ),
        offsets,
        kappa,
        shifts,
        fracs,
        values,
        far_sent,
        scratch=[pltpu.VMEM((BLOCKS, ROWS, LANES), F32)] * 2,
    )
    near = lax.ppermute(near_sent, "gx", swaps(radial_size, 0))
    values = call(
        outer_kernel,
        "outer",
        whole,
        offsets,
        coefs,
        shifts,
        fracs,
        near_sent,
        far_sent,
        partial,
        beyond,
        unfinished,
        middle,
        near,
        far,
        scratch=[pltpu.VMEM((BLOCKS, SIDE_ROWS, LANES), F32)] * 4,
    )
    return unpack(back, across(values))


def solution(mesh):
    placed = (P(None, "gx", None, "gy"), P(None, "gx"), P(None, "gx"), P(), P())
    return jax.shard_map(
        on_device, mesh=mesh, in_specs=placed, out_specs=P(None, "gx", None, "gy"), check_vma=False
    )
```
